256 devices in a mesh: col: 64 (over z, x, core), row: 4 (over y).
Axes of the slice: x: 4, y: 4, z: 8, core: 2. Of those that a mesh axis runs over, the one named last changes fastest.
Arguments:
- amplitudes: bfloat16 [16, 512, 512], P(None, 'col', 'row'), may hold values from -6 to 6
- integrals: bfloat16 [32768, 32768], P('col', 'row'), may hold values from -0.03125 to 0.03125
- partner: int32 [8], replicated, may hold values from 0 to 7, as said below
Outputs:
- ladder: bfloat16 [16, 512, 512], P(None, 'col', 'row')
The draws below stay inside these ranges and needn't reach their ends.
Inputs may be any that keep to these rules, and one draw needn't show every extreme that they name: partner is an involution without fixed points: tile d pairs with the tile whose irrep times d's irrep is the occupied pairs' irrep.
All inputs are finite; a program needn't handle non-finite values.
Results may differ from the reference program's by a relative error of at most 0.001.
Values may be sent and summed in bfloat16 or wider, within the bound.
No kernel may reach another device: no remote copies, remote signals or barrier semaphores. Data moves between devices by JAX's collectives and lax.ppermute only.
A program may use at most 64 MiB of HBM per device.

```python
import jax
import jax.numpy as jnp
from jax import lax

NP = 16
NV = 512
TS = 64
NT = 8
KPAIR = 32768


def draw_partner(key, part):
    key = jax.random.fold_in(key, 5)
    order = jax.random.permutation(key, NT).astype(jnp.int32)
    firsts = order[0::2]
    seconds = order[1::2]
    table = jnp.zeros((NT,), jnp.int32)
    table = table.at[firsts].set(seconds)
    table = table.at[seconds].set(firsts)
    return table.astype(jnp.int32)


def level_of(stream_key, shape, cuts, smallest, top_value):
    factor_of, own = 1.0, jax.random.fold_in(stream_key, 6)
    for dim, parts in cuts:
        heights = jnp.exp(jax.random.uniform(jax.random.fold_in(own, dim), (parts,), jnp.float32, smallest / len(cuts), top_value / len(cuts)))
        factor_of = factor_of * jnp.repeat(heights, shape[dim] // parts).reshape([-1 if axis == dim else 1 for axis in range(len(shape))])
    return factor_of


def bell_draw(own_key, shape, width, most, split=(), kind=jnp.bfloat16):
    factor_of = level_of(own_key, shape, split, -0.22, 0.18) if split else 1.0
    array = jax.random.normal(own_key, shape, jnp.float32) * width * factor_of
    return jnp.minimum(jnp.maximum(array, -most), most).astype(kind)


def setup_inputs(seed: int = 0) -> dict:
    splits = jax.random.split(jax.random.key(seed), 4)
    amplitudes = bell_draw(splits[0], (NP, NV, NV), 1.0, 6.0, ((1, 64), (2, 4)))
    integrals = bell_draw(splits[1], (KPAIR, KPAIR), KPAIR ** -0.5, 0.03125, ((0, 64), (1, 4)))
    partner = draw_partner(jax.random.fold_in(splits[3], 71), 0)
    return dict(amplitudes=amplitudes, integrals=integrals, partner=partner)


def reference(amplitudes, integrals, partner):
    tiles = NV // TS
    pieces = []
    for tile_d in range(tiles):
        start_row = partner[tile_d].astype(jnp.int32) * TS
        pieces.append(lax.dynamic_slice(amplitudes, (jnp.int32(0), start_row, jnp.int32(tile_d * TS)), (NP, TS, TS)))
    packed = jnp.stack(pieces, 1).reshape(NP, KPAIR)
    bra_rows = integrals.reshape(tiles, TS * TS, KPAIR)

    def per_tile(rows):
        return jnp.dot(packed, rows.T, preferred_element_type=jnp.float32)

    blocks = lax.map(per_tile, bra_rows)
    pair_result = blocks.astype(jnp.bfloat16)
    ladder = jnp.zeros((NP, NV, NV), jnp.bfloat16)
    for tile_b in range(tiles):
        start_row = partner[tile_b].astype(jnp.int32) * TS
        piece = pair_result[tile_b].reshape(NP, TS, TS)
        ladder = lax.dynamic_update_slice(ladder, piece, (jnp.int32(0), start_row, jnp.int32(tile_b * TS)))
    return ladder
```

```python
import jax
import jax.numpy as jnp
from jax import lax
from jax.experimental import pallas as pl
from jax.experimental.pallas import tpu as pltpu
from jax.sharding import Mesh
from jax.sharding import PartitionSpec as P

TS = 64
ZH, ZL, X, CORE, ROW = 4, 2, 4, 2, 4
AXES = ("zh", "zl", "x", "core", "row")
REACH = (3, 1, 0, 2)


def target_z(zh, zl, row):
    off = REACH[(row - zh) % ROW]
    return (2 * zh - off) % (ZH * ZL) if zl == 0 else (2 * zh + 1 + off) % (ZH * ZL)


def linear(zh, zl, x, core, row):
    return (((zh * ZL + zl) * X + x) * CORE + core) * ROW + row


def delivery_pairs():
    pairs = []
    for zh in range(ZH):
        for zl in range(ZL):
            for x in range(X):
                for core in range(CORE):
                    for row in range(ROW):
                        t = target_z(zh, zl, row)
                        pairs.append((linear(zh, zl, x, core, row), linear(t // ZL, t % ZL, x, core, zh)))
    return pairs


def matmul_kernel(packed_ref, integrals_ref, out_ref):
    subs, halves, pairs, width = packed_ref.shape
    half_width = subs * width
    total = jnp.zeros((pairs, integrals_ref.shape[0]), jnp.float32)
    for h in range(halves):
        for s in range(subs):
            total = total + lax.dot_general(
                packed_ref[s, h],
                integrals_ref[:, pl.ds(h * half_width + s * width, width)],
                (((1,), (1,)), ((), ())),
                preferred_element_type=jnp.float32,
            )
    for j in range(out_ref.shape[0]):
        out_ref[j] = total


def per_device(amplitudes, integrals, partner):
    zh, zl = lax.axis_index("zh"), lax.axis_index("zl")
    row = lax.axis_index("row")
    z = zh * ZL + zl
    pairs, rows_dev, cols_dev = amplitudes.shape
    width = rows_dev * TS
    tiles = ZH * ZL
    ids = jnp.arange(tiles, dtype=jnp.int32)

    def entry(i):
        return jnp.sum(jnp.where(ids == i, partner, 0))

    half = entry(z) % 2
    mine = jnp.where(half == 0, amplitudes[:, :, :TS], amplitudes[:, :, TS:]).reshape(pairs, width)
    sent = jnp.broadcast_to(mine[None], (tiles, pairs, width))
    got = lax.all_to_all(sent, ("zh", "zl"), 0, 0, tiled=True)
    chosen = jnp.stack(
        [lax.dynamic_slice(got, (entry(2 * row + h), 0, 0), (1, pairs, width))[0] for h in range(2)]
    )
    sent = jnp.broadcast_to(chosen[None], (X * CORE, 2, pairs, width))
    packed = lax.all_to_all(sent, ("x", "core"), 0, 0, tiled=True)
    group = ZL * ROW
    partials = pl.pallas_call(
        matmul_kernel,
        out_shape=jax.ShapeDtypeStruct((group, pairs, integrals.shape[0]), jnp.float32),
        in_specs=[pl.BlockSpec(memory_space=pltpu.VMEM)] * 2,
        out_specs=pl.BlockSpec(memory_space=pltpu.VMEM),
        compiler_params=pltpu.CompilerParams(vmem_limit_bytes=40 * 1024 * 1024),
        name="ladder_matmul",
    )(packed, integrals)
    shared = lax.all_to_all(partials, ("zl", "row"), 0, 0, tiled=True)
    sums = jnp.sum(shared.reshape(ZL, ROW, pairs, width), axis=1)
    off = jnp.array(REACH, jnp.int32)[(row - zh) % ROW]
    target = jnp.where(zl == 0, 2 * zh - off + tiles, 2 * zh + 1 + off) % tiles
    bra = entry(target)
    block = jnp.where(bra % 2 == 0, sums[0], sums[1]).astype(jnp.bfloat16).reshape(pairs, rows_dev, TS)
    useful = bra // 2 == zh
    zero = jnp.zeros_like(block)
    left = jnp.where(useful & (bra % 2 == 0), block, zero)
    right = jnp.where(useful & (bra % 2 == 1), block, zero)
    out = jnp.concatenate([left, right], axis=2)
    return lax.ppermute(out, AXES, delivery_pairs())


def solution(mesh):
    fine = Mesh(mesh.devices.reshape(ZH, ZL, X, CORE, ROW), AXES)
    col = ("zh", "zl", "x", "core")
    return jax.shard_map(
        per_device,
        mesh=fine,
        in_specs=(P(None, col, "row"), P(col, "row"), P()),
        out_specs=P(None, col, "row"),
        check_vma=False,
    )
```

```python
import jax
import jax.numpy as jnp
from jax import lax
from jax.experimental import pallas as pl
from jax.experimental.pallas import tpu as pltpu
from jax.sharding import Mesh
from jax.sharding import PartitionSpec as P

TS = 64
ZH, ZL, X, CORE, ROW = 4, 2, 4, 2, 4
TILES = ZH * ZL
AXES = ("zh", "zl", "x", "core", "row")
PIECES = 8
REACH = (3, 1, 0, 2)
VMEM = pl.BlockSpec(memory_space=pltpu.VMEM)
HBM = pl.BlockSpec(memory_space=pltpu.HBM)


def target_z(zh, zl, row):
    off = REACH[(row - zh) % ROW]
    return (2 * zh - off) % TILES if zl == 0 else (2 * zh + 1 + off) % TILES


def linear(zh, zl, x, core, row):
    return (((zh * ZL + zl) * X + x) * CORE + core) * ROW + row


def delivery_pairs():
    pairs = []
    for zh in range(ZH):
        for zl in range(ZL):
            for x in range(X):
                for core in range(CORE):
                    for row in range(ROW):
                        t = target_z(zh, zl, row)
                        pairs.append((linear(zh, zl, x, core, row), linear(t // ZL, t % ZL, x, core, zh)))
    return pairs


def in_vmem(x):
    return pltpu.with_memory_space_constraint(x, pltpu.VMEM)


def in_hbm(x):
    return pltpu.with_memory_space_constraint(x, pltpu.HBM)


def lower_lanes(rows):
    return lax.broadcasted_iota(jnp.int32, (rows, 2 * TS), 1) < TS


def fetch(copies):
    for copy in copies:
        copy.start()
    for copy in copies:
        copy.wait()


def prepare_kernel(partner_hbm, amplitudes_hbm, sent_ref, pick_ref, keep_ref, partner_ref, amplitudes_ref, sems):
    fetch(
        [
            pltpu.make_async_copy(partner_hbm, partner_ref, sems.at[0]),
            pltpu.make_async_copy(amplitudes_hbm, amplitudes_ref, sems.at[1]),
        ]
    )
    zh, zl, row = lax.axis_index("zh"), lax.axis_index("zl"), lax.axis_index("row")
    for h in range(2):
        source = partner_ref[2 * row + h]
        for z in range(TILES):
            pick_ref[h, z] = jnp.full(pick_ref.shape[2:], jnp.where(source == z, 1, 0), jnp.int32)
    turn = (row - zh + ROW) % ROW
    off = jnp.where(turn == 0, REACH[0], jnp.where(turn == 1, REACH[1], jnp.where(turn == 2, REACH[2], REACH[3])))
    target = jnp.where(zl == 0, 2 * zh - off + TILES, 2 * zh + 1 + off) % TILES
    bra = partner_ref[target]
    for h in range(2):
        keep_ref[h] = jnp.full(keep_ref.shape[1:], jnp.where(bra == 2 * zh + h, 1, 0), jnp.int32)
    z = zh * ZL + zl
    upper = partner_ref[z] % 2 == 1
    rows = jnp.swapaxes(amplitudes_ref[...].astype(jnp.float32), 0, 1)
    units, pairs, _ = rows.shape
    lower = lower_lanes(pairs)
    columns = []
    for j in range(units // 2):
        first, second = rows[2 * j], rows[2 * j + 1]
        from_lower = jnp.where(lower, first, pltpu.roll(second, TS, 1))
        from_upper = jnp.where(lower, pltpu.roll(first, TS, 1), second)
        columns.append(jnp.where(upper, from_upper, from_lower))
    mine = jnp.concatenate(columns, axis=1).astype(sent_ref.dtype)
    for j in range(sent_ref.shape[0]):
        sent_ref[j] = mine


def choose_kernel(pick_ref, got_ref, chosen_ref):
    tiles, pairs, width = got_ref.shape
    reps = width // pick_ref.shape[3]
    for h in range(2):
        chosen = jnp.zeros((pairs, width), jnp.float32)
        for z in range(tiles):
            wanted = jnp.concatenate([pick_ref[h, z]] * reps, axis=1) != 0
            chosen = jnp.where(wanted, got_ref[z].astype(jnp.float32), chosen)
        chosen_ref[h] = chosen.astype(chosen_ref.dtype)


def stage_kernel(integrals_ref, staged_ref, sems):
    step = integrals_ref.shape[0] // PIECES
    parts = [pl.ds(j * step, step) for j in range(PIECES)]
    fetch([pltpu.make_async_copy(integrals_ref.at[p, :], staged_ref.at[p, :], sems.at[j]) for j, p in enumerate(parts)])


def product(packed_ref, integrals_ref, core, places):
    width = packed_ref.shape[3]
    total = jnp.zeros((packed_ref.shape[2], integrals_ref.shape[0]), jnp.float32)
    for i, x in enumerate(places):
        for h in range(2):
            start = pl.multiple_of(((h * X + x) * CORE + core) * width, width)
            total = total + lax.dot_general(
                packed_ref[i, h],
                integrals_ref[:, pl.ds(start, width)],
                (((1,), (1,)), ((), ())),
                preferred_element_type=jnp.float32,
            )
    return total


def join_kernel(first_ref, second_ref, *rest):
    out_ref = rest[-1]
    count = first_ref.shape[0]
    out_ref[pl.ds(0, count)] = first_ref[...]
    out_ref[pl.ds(count, count)] = second_ref[...]


def near(x):
    return x + 1 - 2 * (x % 2)


def near_kernel(packed_ref, integrals_ref, out_ref):
    x = lax.axis_index("x")
    out_ref[...] = product(packed_ref, integrals_ref, lax.axis_index("core"), [x, near(x)])


def far_kernel(packed_ref, before_ref, integrals_ref, out_ref):
    x = X - 1 - lax.axis_index("x")
    out_ref[...] = before_ref[...] + product(packed_ref, integrals_ref, lax.axis_index("core"), [x, near(x)])


def other_kernel(packed_ref, before_ref, integrals_ref, out_ref):
    x = lax.axis_index("x")
    y = X - 1 - x
    places = [x, near(x), y, near(y)]
    total = before_ref[...] + product(packed_ref, integrals_ref, 1 - lax.axis_index("core"), places)
    for j in range(out_ref.shape[0]):
        out_ref[j] = total


def finish_kernel(keep_ref, shared_ref, out_ref):
    pairs, width = shared_ref.shape[1:]
    sums = []
    for h in range(2):
        total = shared_ref[h * ROW]
        for j in range(1, ROW):
            total = total + shared_ref[h * ROW + j]
        wanted = jnp.concatenate([keep_ref[h]] * (width // keep_ref.shape[2]), axis=1) != 0
        total = jnp.where(wanted, total, 0.0)
        sums.append(total.astype(jnp.bfloat16).astype(jnp.float32))
    lower = lower_lanes(pairs)
    rows = []
    for j in range(width // (2 * TS)):
        part = slice(j * 2 * TS, (j + 1) * 2 * TS)
        left, right = sums[0][:, part], sums[1][:, part]
        rows.append(jnp.where(lower, left, pltpu.roll(right, TS, 1)))
        rows.append(jnp.where(lower, pltpu.roll(left, TS, 1), right))
    out_ref[...] = jnp.swapaxes(jnp.stack(rows, 0), 0, 1).astype(out_ref.dtype)


def per_device(amplitudes, integrals, partner):
    pairs, rows_dev, _ = amplitudes.shape
    width = rows_dev * TS
    bra = integrals.shape[0]
    params = pltpu.CompilerParams(vmem_limit_bytes=4 * 1024 * 1024)
    sent, pick, keep = pl.pallas_call(
        prepare_kernel,
        out_shape=[
            pltpu.VMEM((TILES, pairs, width), jnp.bfloat16),
            pltpu.VMEM((2, TILES, pairs, 128), jnp.int32),
            pltpu.VMEM((2, pairs, 128), jnp.int32),
        ],
        in_specs=[HBM, HBM],
        out_specs=[VMEM, VMEM, VMEM],
        scratch_shapes=[
            pltpu.SMEM(partner.shape, partner.dtype),
            pltpu.VMEM(amplitudes.shape, amplitudes.dtype),
            pltpu.SemaphoreType.DMA((2,)),
        ],
        compiler_params=params,
        name="prepare",
    )(in_hbm(partner), in_hbm(amplitudes))
    got = lax.all_to_all(sent, ("zh", "zl"), 0, 0, tiled=True)
    chosen = pl.pallas_call(
        choose_kernel,
        out_shape=pltpu.VMEM((2, pairs, width), jnp.bfloat16),
        in_specs=[VMEM, VMEM],
        out_specs=VMEM,
        compiler_params=params,
        name="choose",
    )(in_vmem(pick), in_vmem(got))
    staged = pl.pallas_call(
        stage_kernel,
        out_shape=pltpu.VMEM(integrals.shape, integrals.dtype),
        in_specs=[HBM],
        out_specs=VMEM,
        scratch_shapes=[pltpu.SemaphoreType.DMA((PIECES,))],
        compiler_params=params,
        cost_estimate=pl.CostEstimate(flops=0, bytes_accessed=2 * integrals.size, transcendentals=0),
        name="stage",
    )(in_hbm(integrals))

    def multiply(kernel, operands, share, copies, name):
        shape = (pairs, bra) if copies == 1 else (copies, pairs, bra)
        operands = [*operands, staged]
        return pl.pallas_call(
            kernel,
            out_shape=pltpu.VMEM(shape, jnp.float32),
            in_specs=[VMEM] * len(operands),
            out_specs=VMEM,
            compiler_params=params,
            cost_estimate=pl.CostEstimate(
                flops=2 * pairs * integrals.size // share,
                bytes_accessed=2 * integrals.size // share,
                transcendentals=0,
            ),
            name=name,
        )(*[in_vmem(operand) for operand in operands])

    def join(operands):
        first = operands[0]
        return pl.pallas_call(
            join_kernel,
            out_shape=pltpu.VMEM((2 * first.shape[0], *first.shape[1:]), first.dtype),
            in_specs=[VMEM, VMEM, VMEM],
            out_specs=VMEM,
            compiler_params=params,
            name="join",
        )(*[in_vmem(operand) for operand in operands])

    beside = lax.ppermute(chosen, "x", [(i, i ^ 1) for i in range(X)])
    couple = join([chosen[None], beside[None], staged])
    across = lax.ppermute(couple, "x", [(i, X - 1 - i) for i in range(X)])
    total = multiply(near_kernel, [couple], 4, 1, "near_product")
    four = join([couple, across, total])
    neighbour = lax.ppermute(four, "core", [(0, 1), (1, 0)])
    total = multiply(far_kernel, [across, total], 4, 1, "far_product")
    partials = multiply(other_kernel, [neighbour, total], 2, ZL * ROW, "other_product")
    shared = lax.all_to_all(partials, ("zl", "row"), 0, 0, tiled=True)
    out = pl.pallas_call(
        finish_kernel,
        out_shape=pltpu.VMEM(amplitudes.shape, jnp.bfloat16),
        in_specs=[VMEM, VMEM],
        out_specs=VMEM,
        compiler_params=params,
        name="finish",
    )(in_vmem(keep), in_vmem(shared))
    return lax.ppermute(out, AXES, delivery_pairs())


def solution(mesh):
    fine = Mesh(mesh.devices.reshape(ZH, ZL, X, CORE, ROW), AXES)
    col = ("zh", "zl", "x", "core")
    return jax.shard_map(
        per_device,
        mesh=fine,
        in_specs=(P(None, col, "row"), P(col, "row"), P()),
        out_specs=P(None, col, "row"),
        check_vma=False,
    )
```

```python
import jax
import jax.numpy as jnp
from jax import lax
from jax.experimental import pallas as pl
from jax.experimental.pallas import tpu as pltpu
from jax.sharding import Mesh
from jax.sharding import PartitionSpec as P

TS = 64
ZH, ZL, X, CORE, ROW = 4, 2, 4, 2, 4
TILES = ZH * ZL
AXES = ("zh", "zl", "x", "core", "row")
PIECES = 8
REACH = (3, 1, 0, 2)
VMEM = pl.BlockSpec(memory_space=pltpu.VMEM)
HBM = pl.BlockSpec(memory_space=pltpu.HBM)


def target_z(zh, zl, row):
    off = REACH[(row - zh) % ROW]
    return (2 * zh - off) % TILES if zl == 0 else (2 * zh + 1 + off) % TILES


def linear(zh, zl, x, core, row):
    return (((zh * ZL + zl) * X + x) * CORE + core) * ROW + row


def delivery_pairs():
    pairs = []
    for zh in range(ZH):
        for zl in range(ZL):
            for x in range(X):
                for core in range(CORE):
                    for row in range(ROW):
                        t = target_z(zh, zl, row)
                        pairs.append((linear(zh, zl, x, core, row), linear(t // ZL, t % ZL, x, core, zh)))
    return pairs


def in_vmem(x):
    return pltpu.with_memory_space_constraint(x, pltpu.VMEM)


def in_hbm(x):
    return pltpu.with_memory_space_constraint(x, pltpu.HBM)


def lower_lanes(rows):
    return lax.broadcasted_iota(jnp.int32, (rows, 2 * TS), 1) < TS


def fetch(copies):
    for copy in copies:
        copy.start()
    for copy in copies:
        copy.wait()


def prepare_kernel(partner_hbm, amplitudes_hbm, sent_ref, pick_ref, keep_ref, partner_ref, amplitudes_ref, sems):
    fetch(
        [
            pltpu.make_async_copy(partner_hbm, partner_ref, sems.at[0]),
            pltpu.make_async_copy(amplitudes_hbm, amplitudes_ref, sems.at[1]),
        ]
    )
    zh, zl, row = lax.axis_index("zh"), lax.axis_index("zl"), lax.axis_index("row")
    for h in range(2):
        source = partner_ref[2 * row + h]
        for z in range(TILES):
            pick_ref[h, z] = jnp.full(pick_ref.shape[2:], jnp.where(source == z, 1, 0), jnp.int32)
    turn = (row - zh + ROW) % ROW
    off = jnp.where(turn == 0, REACH[0], jnp.where(turn == 1, REACH[1], jnp.where(turn == 2, REACH[2], REACH[3])))
    target = jnp.where(zl == 0, 2 * zh - off + TILES, 2 * zh + 1 + off) % TILES
    bra = partner_ref[target]
    for h in range(2):
        keep_ref[h] = jnp.full(keep_ref.shape[1:], jnp.where(bra == 2 * zh + h, 1, 0), jnp.int32)
    z = zh * ZL + zl
    upper = partner_ref[z] % 2 == 1
    rows = jnp.swapaxes(amplitudes_ref[...].astype(jnp.float32), 0, 1)
    units, pairs, _ = rows.shape
    lower = lower_lanes(pairs)
    columns = []
    for j in range(units // 2):
        first, second = rows[2 * j], rows[2 * j + 1]
        from_lower = jnp.where(lower, first, pltpu.roll(second, TS, 1))
        from_upper = jnp.where(lower, pltpu.roll(first, TS, 1), second)
        columns.append(jnp.where(upper, from_upper, from_lower))
    mine = jnp.concatenate(columns, axis=1).astype(sent_ref.dtype)
    for j in range(sent_ref.shape[0]):
        sent_ref[j] = mine


def choose_kernel(pick_ref, got_ref, chosen_ref):
    tiles, pairs, width = got_ref.shape
    reps = width // pick_ref.shape[3]
    for h in range(2):
        chosen = jnp.zeros((pairs, width), jnp.float32)
        for z in range(tiles):
            wanted = jnp.concatenate([pick_ref[h, z]] * reps, axis=1) != 0
            chosen = jnp.where(wanted, got_ref[z].astype(jnp.float32), chosen)
        chosen_ref[h] = chosen.astype(chosen_ref.dtype)


def stage_top_kernel(integrals_ref, staged_ref, sems):
    step = staged_ref.shape[0] // PIECES
    parts = [pl.ds(j * step, step) for j in range(PIECES)]
    fetch([pltpu.make_async_copy(integrals_ref.at[p, :], staged_ref.at[p, :], sems.at[j]) for j, p in enumerate(parts)])


def join_kernel(first_ref, second_ref, *rest):
    out_ref = rest[-1]
    count = first_ref.shape[0]
    out_ref[pl.ds(0, count)] = first_ref[...]
    out_ref[pl.ds(count, count)] = second_ref[...]


def after_kernel(value_ref, first_ref, out_ref):
    out_ref[...] = value_ref[...]


def partial_product(packed_ref, integrals_ref, core, x):
    width = packed_ref.shape[3]
    places = [x, x + 1 - 2 * (x % 2)]
    total = jnp.zeros((packed_ref.shape[2], integrals_ref.shape[0]), jnp.float32)
    for i, place in enumerate(places):
        for h in range(2):
            start = pl.multiple_of(((h * X + place) * CORE + core) * width, width)
            total = total + lax.dot_general(
                packed_ref[i, h],
                integrals_ref[:, pl.ds(start, width)],
                (((1,), (1,)), ((), ())),
                preferred_element_type=jnp.float32,
            )
    return total


def product(packed_ref, top_ref, bottom_ref, core, x):
    return jnp.concatenate([partial_product(packed_ref, ref, core, x) for ref in (top_ref, bottom_ref)], axis=1)


def near_kernel(packed_ref, swapped_ref, top_ref, integrals_ref, bottom_ref, out_ref, sems):
    core, x = lax.axis_index("core"), lax.axis_index("x")
    rows, columns = bottom_ref.shape
    span = columns // 4
    copies = []
    for n in range(2):
        pair = (x // 2 + n) % 2
        for h in range(2):
            part = pl.ds(pl.multiple_of((2 * h + pair) * span, span), span)
            source = integrals_ref.at[pl.ds(rows, rows), part]
            copy = pltpu.make_async_copy(source, bottom_ref.at[:, part], sems.at[len(copies)])
            copy.start()
            copies.append(copy)

    def both(ref):
        return partial_product(packed_ref, ref, core, x) + partial_product(swapped_ref, ref, 1 - core, x)

    @pl.when(core >= 0)
    def _():
        out_ref[:, pl.ds(0, rows)] = both(top_ref)

    for copy in copies[:2]:
        copy.wait()

    @pl.when(x >= 0)
    def _():
        out_ref[:, pl.ds(rows, rows)] = both(bottom_ref)

    for copy in copies[2:]:
        copy.wait()


def far_kernel(packed_ref, before_ref, top_ref, bottom_ref, out_ref):
    core, x = lax.axis_index("core"), X - 1 - lax.axis_index("x")
    out_ref[...] = before_ref[...] + product(packed_ref, top_ref, bottom_ref, core, x)


def last_kernel(packed_ref, before_ref, top_ref, bottom_ref, out_ref):
    core, x = 1 - lax.axis_index("core"), X - 1 - lax.axis_index("x")
    total = before_ref[...] + product(packed_ref, top_ref, bottom_ref, core, x)
    for j in range(out_ref.shape[0]):
        out_ref[j] = total


def finish_kernel(keep_ref, shared_ref, out_ref):
    pairs, width = shared_ref.shape[1:]
    sums = []
    for h in range(2):
        total = shared_ref[h * ROW]
        for j in range(1, ROW):
            total = total + shared_ref[h * ROW + j]
        wanted = jnp.concatenate([keep_ref[h]] * (width // keep_ref.shape[2]), axis=1) != 0
        total = jnp.where(wanted, total, 0.0)
        sums.append(total.astype(jnp.bfloat16).astype(jnp.float32))
    lower = lower_lanes(pairs)
    rows = []
    for j in range(width // (2 * TS)):
        part = slice(j * 2 * TS, (j + 1) * 2 * TS)
        left, right = sums[0][:, part], sums[1][:, part]
        rows.append(jnp.where(lower, left, pltpu.roll(right, TS, 1)))
        rows.append(jnp.where(lower, pltpu.roll(left, TS, 1), right))
    out_ref[...] = jnp.swapaxes(jnp.stack(rows, 0), 0, 1).astype(out_ref.dtype)


def per_device(amplitudes, integrals, partner):
    pairs, rows_dev, _ = amplitudes.shape
    width = rows_dev * TS
    bra = integrals.shape[0]
    params = pltpu.CompilerParams(vmem_limit_bytes=4 * 1024 * 1024)
    sent, pick, keep = pl.pallas_call(
        prepare_kernel,
        out_shape=[
            pltpu.VMEM((TILES, pairs, width), jnp.bfloat16),
            pltpu.VMEM((2, TILES, pairs, 128), jnp.int32),
            pltpu.VMEM((2, pairs, 128), jnp.int32),
        ],
        in_specs=[HBM, HBM],
        out_specs=[VMEM, VMEM, VMEM],
        scratch_shapes=[
            pltpu.SMEM(partner.shape, partner.dtype),
            pltpu.VMEM(amplitudes.shape, amplitudes.dtype),
            pltpu.SemaphoreType.DMA((2,)),
        ],
        compiler_params=params,
        name="prepare",
    )(in_hbm(partner), in_hbm(amplitudes))
    got = lax.all_to_all(sent, ("zh", "zl"), 0, 0, tiled=True)
    chosen = pl.pallas_call(
        choose_kernel,
        out_shape=pltpu.VMEM((2, pairs, width), jnp.bfloat16),
        in_specs=[VMEM, VMEM],
        out_specs=VMEM,
        compiler_params=params,
        name="choose",
    )(in_vmem(pick), in_vmem(got))
    staged = pltpu.VMEM((bra // 2, integrals.shape[1]), integrals.dtype)

    def local(kernel, shape, dtype, operands, cost=None, name=None, scratch=(), specs=None):
        return pl.pallas_call(
            kernel,
            out_shape=pltpu.VMEM(shape, dtype),
            in_specs=specs or [VMEM] * len(operands),
            out_specs=VMEM,
            scratch_shapes=scratch,
            compiler_params=params,
            cost_estimate=cost,
            name=name,
        )(*operands)

    def multiply(kernel, operands, name, copies=()):
        cost = pl.CostEstimate(
            flops=pairs * integrals.size // 2, bytes_accessed=integrals.size // 2, transcendentals=0
        )
        operands = [in_vmem(operand) for operand in operands]
        return local(kernel, (*copies, pairs, bra), jnp.float32, operands, cost, name)

    core_swap = [(0, 1), (1, 0)]
    beside = lax.ppermute(chosen, "x", [(i, i ^ 1) for i in range(X)])
    top = pl.pallas_call(
        stage_top_kernel,
        out_shape=staged,
        in_specs=[HBM],
        out_specs=VMEM,
        scratch_shapes=[pltpu.SemaphoreType.DMA((PIECES,))],
        compiler_params=params,
        cost_estimate=pl.CostEstimate(flops=0, bytes_accessed=2 * integrals.size, transcendentals=0),
        name="stage_top",
    )(in_hbm(integrals))
    couple = local(
        join_kernel,
        (2, 2, pairs, width),
        chosen.dtype,
        [in_vmem(chosen[None]), in_vmem(beside[None]), in_vmem(top)],
        name="join",
    )
    swapped = lax.ppermute(couple, "core", core_swap)
    across = lax.ppermute(couple, "x", [(i, X - 1 - i) for i in range(X)])
    bottom, total = pl.pallas_call(
        near_kernel,
        out_shape=[staged, pltpu.VMEM((pairs, bra), jnp.float32)],
        in_specs=[VMEM, VMEM, VMEM, HBM],
        out_specs=[VMEM, VMEM],
        scratch_shapes=[pltpu.SemaphoreType.DMA((PIECES,))],
        compiler_params=params,
        cost_estimate=pl.CostEstimate(
            flops=pairs * integrals.size, bytes_accessed=2 * integrals.size, transcendentals=0
        ),
        name="near_product",
    )(in_vmem(couple), in_vmem(swapped), in_vmem(top), in_hbm(integrals))
    across = local(after_kernel, across.shape, across.dtype, [in_vmem(across), in_vmem(total)], name="after")
    swapped = lax.ppermute(across, "core", core_swap)
    total = multiply(far_kernel, [across, total, top, bottom], "far_product")
    partials = multiply(last_kernel, [swapped, total, top, bottom], "last_product", (ZL * ROW,))
    shared = lax.all_to_all(partials, ("zl", "row"), 0, 0, tiled=True)
    out = pl.pallas_call(
        finish_kernel,
        out_shape=pltpu.VMEM(amplitudes.shape, jnp.bfloat16),
        in_specs=[VMEM, VMEM],
        out_specs=VMEM,
        compiler_params=params,
        name="finish",
    )(in_vmem(keep), in_vmem(shared))
    return lax.ppermute(out, AXES, delivery_pairs())


def solution(mesh):
    fine = Mesh(mesh.devices.reshape(ZH, ZL, X, CORE, ROW), AXES)
    col = ("zh", "zl", "x", "core")
    return jax.shard_map(
        per_device,
        mesh=fine,
        in_specs=(P(None, col, "row"), P(col, "row"), P()),
        out_specs=P(None, col, "row"),
        check_vma=False,
    )
```

```python
import jax
import jax.numpy as jnp
from jax import lax
from jax.experimental import pallas as pl
from jax.experimental.pallas import tpu as pltpu
from jax.sharding import Mesh
from jax.sharding import PartitionSpec as P

TS = 64
ZH, ZL, X, CORE, ROW = 4, 2, 4, 2, 4
TILES = ZH * ZL
AXES = ("zh", "zl", "x", "core", "row")
PIECES = 8
REACH = (3, 0, 1, 2)
VMEM = pl.BlockSpec(memory_space=pltpu.VMEM)
HBM = pl.BlockSpec(memory_space=pltpu.HBM)


def target_z(zh, zl, row):
    off = REACH[(row - zh) % ROW]
    return (2 * zh - off) % TILES if zl == 0 else (2 * zh + 1 + off) % TILES


def linear(zh, zl, x, core, row):
    return (((zh * ZL + zl) * X + x) * CORE + core) * ROW + row


def delivery_pairs():
    pairs = []
    for zh in range(ZH):
        for zl in range(ZL):
            for x in range(X):
                for core in range(CORE):
                    for row in range(ROW):
                        t = target_z(zh, zl, row)
                        pairs.append((linear(zh, zl, x, core, row), linear(t // ZL, t % ZL, x, core, zh)))
    return pairs


def in_vmem(x):
    return pltpu.with_memory_space_constraint(x, pltpu.VMEM)


def in_hbm(x):
    return pltpu.with_memory_space_constraint(x, pltpu.HBM)


def lower_lanes(rows):
    return lax.broadcasted_iota(jnp.int32, (rows, 2 * TS), 1) < TS


def fetch(copies):
    for copy in copies:
        copy.start()
    for copy in copies:
        copy.wait()


def prepare_kernel(
    partner_hbm, amplitudes_hbm, sent_ref, pick_ref, odd_ref, place_ref, partner_ref, amplitudes_ref, sems
):
    fetch(
        [
            pltpu.make_async_copy(partner_hbm, partner_ref, sems.at[0]),
            pltpu.make_async_copy(amplitudes_hbm, amplitudes_ref, sems.at[1]),
        ]
    )
    zh, zl, row = lax.axis_index("zh"), lax.axis_index("zl"), lax.axis_index("row")
    for h in range(2):
        source = partner_ref[2 * row + h]
        for z in range(TILES):
            pick_ref[h, z] = jnp.full(pick_ref.shape[2:], jnp.where(source == z, 1, 0), jnp.int32)
    turn = (row - zh + ROW) % ROW
    off = jnp.where(turn == 0, REACH[0], jnp.where(turn == 1, REACH[1], jnp.where(turn == 2, REACH[2], REACH[3])))
    target = jnp.where(zl == 0, 2 * zh - off + TILES, 2 * zh + 1 + off) % TILES
    bra = partner_ref[target]
    odd_ref[...] = jnp.full(odd_ref.shape, bra % 2, jnp.int32)
    z = zh * ZL + zl
    for h in range(2):
        place_ref[h] = jnp.full(place_ref.shape[1:], jnp.where(partner_ref[z] == 2 * row + h, 1, 0), jnp.int32)
    upper = partner_ref[z] % 2 == 1
    rows = jnp.swapaxes(amplitudes_ref[...].astype(jnp.float32), 0, 1)
    units, pairs, _ = rows.shape
    lower = lower_lanes(pairs)
    columns = []
    for j in range(units // 2):
        first, second = rows[2 * j], rows[2 * j + 1]
        from_lower = jnp.where(lower, first, pltpu.roll(second, TS, 1))
        from_upper = jnp.where(lower, pltpu.roll(first, TS, 1), second)
        columns.append(jnp.where(upper, from_upper, from_lower))
    mine = jnp.concatenate(columns, axis=1).astype(sent_ref.dtype)
    for j in range(sent_ref.shape[0]):
        sent_ref[j] = mine


def choose_kernel(pick_ref, got_ref, chosen_ref):
    tiles, pairs, width = got_ref.shape
    reps = width // pick_ref.shape[3]
    for h in range(2):
        chosen = jnp.zeros((pairs, width), jnp.float32)
        for z in range(tiles):
            wanted = jnp.concatenate([pick_ref[h, z]] * reps, axis=1) != 0
            chosen = jnp.where(wanted, got_ref[z].astype(jnp.float32), chosen)
        chosen_ref[h] = chosen.astype(chosen_ref.dtype)


def stage_top_kernel(integrals_ref, staged_ref, sems):
    step = staged_ref.shape[0] // PIECES
    parts = [pl.ds(j * step, step) for j in range(PIECES)]
    fetch([pltpu.make_async_copy(integrals_ref.at[p, :], staged_ref.at[p, :], sems.at[j]) for j, p in enumerate(parts)])


def join_kernel(first_ref, second_ref, *rest):
    out_ref = rest[-1]
    count = first_ref.shape[0]
    out_ref[pl.ds(0, count)] = first_ref[...]
    out_ref[pl.ds(count, count)] = second_ref[...]


def after_kernel(value_ref, first_ref, out_ref):
    out_ref[...] = value_ref[...]


def partial_product(packed_ref, integrals_ref, core, x):
    width = packed_ref.shape[3]
    places = [x, x + 1 - 2 * (x % 2)]
    total = jnp.zeros((packed_ref.shape[2], integrals_ref.shape[0]), jnp.float32)
    for i, place in enumerate(places):
        for h in range(2):
            start = pl.multiple_of(((h * X + place) * CORE + core) * width, width)
            total = total + lax.dot_general(
                packed_ref[i, h],
                integrals_ref[:, pl.ds(start, width)],
                (((1,), (1,)), ((), ())),
                preferred_element_type=jnp.float32,
            )
    return total


def product(packed_ref, top_ref, bottom_ref, core, x):
    return jnp.concatenate([partial_product(packed_ref, ref, core, x) for ref in (top_ref, bottom_ref)], axis=1)


def near_kernel(packed_ref, swapped_ref, top_ref, integrals_ref, bottom_ref, out_ref, sems):
    core, x = lax.axis_index("core"), lax.axis_index("x")
    rows, columns = bottom_ref.shape
    span = columns // 4
    copies = []
    for n in range(2):
        pair = (x // 2 + n) % 2
        for h in range(2):
            part = pl.ds(pl.multiple_of((2 * h + pair) * span, span), span)
            source = integrals_ref.at[pl.ds(rows, rows), part]
            copy = pltpu.make_async_copy(source, bottom_ref.at[:, part], sems.at[len(copies)])
            copy.start()
            copies.append(copy)

    def both(ref):
        return partial_product(packed_ref, ref, core, x) + partial_product(swapped_ref, ref, 1 - core, x)

    @pl.when(core >= 0)
    def _():
        out_ref[:, pl.ds(0, rows)] = both(top_ref)

    for copy in copies[:2]:
        copy.wait()

    @pl.when(x >= 0)
    def _():
        out_ref[:, pl.ds(rows, rows)] = both(bottom_ref)

    for copy in copies[2:]:
        copy.wait()


def far_kernel(packed_ref, before_ref, top_ref, bottom_ref, out_ref):
    core, x = lax.axis_index("core"), X - 1 - lax.axis_index("x")
    out_ref[...] = before_ref[...] + product(packed_ref, top_ref, bottom_ref, core, x)


def last_kernel(packed_ref, before_ref, top_ref, bottom_ref, out_ref):
    core, x = 1 - lax.axis_index("core"), X - 1 - lax.axis_index("x")
    total = before_ref[...] + product(packed_ref, top_ref, bottom_ref, core, x)
    for j in range(out_ref.shape[0]):
        out_ref[j] = total


def finish_kernel(odd_ref, shared_ref, out_ref):
    odd = jnp.concatenate([odd_ref[...]] * (out_ref.shape[1] // odd_ref.shape[1]), axis=1) != 0
    sums = []
    for h in range(2):
        total = shared_ref[h * ROW]
        for j in range(1, ROW):
            total = total + shared_ref[h * ROW + j]
        sums.append(total)
    out_ref[...] = jnp.where(odd, sums[1], sums[0]).astype(out_ref.dtype)


def place_kernel(place_ref, block_ref, out_ref):
    block = block_ref[...].astype(jnp.float32)
    pairs, width = block.shape
    lower = lower_lanes(pairs)
    left = lower & (place_ref[0] != 0)
    right = jnp.logical_not(lower) & (place_ref[1] != 0)
    rows = []
    for j in range(width // (2 * TS)):
        part = block[:, j * 2 * TS : (j + 1) * 2 * TS]
        turned = pltpu.roll(part, TS, 1)
        rows.append(jnp.where(left, part, jnp.where(right, turned, 0.0)))
        rows.append(jnp.where(left, turned, jnp.where(right, part, 0.0)))
    out_ref[...] = jnp.swapaxes(jnp.stack(rows, 0), 0, 1).astype(out_ref.dtype)


def per_device(amplitudes, integrals, partner):
    pairs, rows_dev, _ = amplitudes.shape
    width = rows_dev * TS
    bra = integrals.shape[0]
    params = pltpu.CompilerParams(vmem_limit_bytes=4 * 1024 * 1024)
    sent, pick, odd, place = pl.pallas_call(
        prepare_kernel,
        out_shape=[
            pltpu.VMEM((TILES, pairs, width), jnp.bfloat16),
            pltpu.VMEM((2, TILES, pairs, 128), jnp.int32),
            pltpu.VMEM((pairs, 128), jnp.int32),
            pltpu.VMEM((2, pairs, 128), jnp.int32),
        ],
        in_specs=[HBM, HBM],
        out_specs=[VMEM, VMEM, VMEM, VMEM],
        scratch_shapes=[
            pltpu.SMEM(partner.shape, partner.dtype),
            pltpu.VMEM(amplitudes.shape, amplitudes.dtype),
            pltpu.SemaphoreType.DMA((2,)),
        ],
        compiler_params=params,
        name="prepare",
    )(in_hbm(partner), in_hbm(amplitudes))
    got = lax.all_to_all(sent, ("zh", "zl"), 0, 0, tiled=True)
    chosen = pl.pallas_call(
        choose_kernel,
        out_shape=pltpu.VMEM((2, pairs, width), jnp.bfloat16),
        in_specs=[VMEM, VMEM],
        out_specs=VMEM,
        compiler_params=params,
        name="choose",
    )(in_vmem(pick), in_vmem(got))
    staged = pltpu.VMEM((bra // 2, integrals.shape[1]), integrals.dtype)

    def local(kernel, shape, dtype, operands, cost=None, name=None, scratch=(), specs=None):
        return pl.pallas_call(
            kernel,
            out_shape=pltpu.VMEM(shape, dtype),
            in_specs=specs or [VMEM] * len(operands),
            out_specs=VMEM,
            scratch_shapes=scratch,
            compiler_params=params,
            cost_estimate=cost,
            name=name,
        )(*operands)

    def multiply(kernel, operands, name, copies=()):
        cost = pl.CostEstimate(
            flops=pairs * integrals.size // 2, bytes_accessed=integrals.size // 2, transcendentals=0
        )
        operands = [in_vmem(operand) for operand in operands]
        return local(kernel, (*copies, pairs, bra), jnp.float32, operands, cost, name)

    core_swap = [(0, 1), (1, 0)]
    beside = lax.ppermute(chosen, "x", [(i, i ^ 1) for i in range(X)])
    top = pl.pallas_call(
        stage_top_kernel,
        out_shape=staged,
        in_specs=[HBM],
        out_specs=VMEM,
        scratch_shapes=[pltpu.SemaphoreType.DMA((PIECES,))],
        compiler_params=params,
        cost_estimate=pl.CostEstimate(flops=0, bytes_accessed=2 * integrals.size, transcendentals=0),
        name="stage_top",
    )(in_hbm(integrals))
    couple = local(
        join_kernel,
        (2, 2, pairs, width),
        chosen.dtype,
        [in_vmem(chosen[None]), in_vmem(beside[None]), in_vmem(top)],
        name="join",
    )
    swapped = lax.ppermute(couple, "core", core_swap)
    across = lax.ppermute(couple, "x", [(i, X - 1 - i) for i in range(X)])
    bottom, total = pl.pallas_call(
        near_kernel,
        out_shape=[staged, pltpu.VMEM((pairs, bra), jnp.float32)],
        in_specs=[VMEM, VMEM, VMEM, HBM],
        out_specs=[VMEM, VMEM],
        scratch_shapes=[pltpu.SemaphoreType.DMA((PIECES,))],
        compiler_params=params,
        cost_estimate=pl.CostEstimate(
            flops=pairs * integrals.size, bytes_accessed=2 * integrals.size, transcendentals=0
        ),
        name="near_product",
    )(in_vmem(couple), in_vmem(swapped), in_vmem(top), in_hbm(integrals))
    across = local(after_kernel, across.shape, across.dtype, [in_vmem(across), in_vmem(total)], name="after")
    swapped = lax.ppermute(across, "core", core_swap)
    total = multiply(far_kernel, [across, total, top, bottom], "far_product")
    partials = multiply(last_kernel, [swapped, total, top, bottom], "last_product", (ZL * ROW,))
    shared = lax.all_to_all(partials, ("zl", "row"), 0, 0, tiled=True)
    block = pl.pallas_call(
        finish_kernel,
        out_shape=pltpu.VMEM((pairs, bra), jnp.bfloat16),
        in_specs=[VMEM, VMEM],
        out_specs=VMEM,
        compiler_params=params,
        name="finish",
    )(in_vmem(odd), in_vmem(shared))
    block = lax.ppermute(block, AXES, delivery_pairs())
    return pl.pallas_call(
        place_kernel,
        out_shape=jax.ShapeDtypeStruct(amplitudes.shape, jnp.bfloat16),
        in_specs=[VMEM, VMEM],
        out_specs=VMEM,
        compiler_params=params,
        name="place",
    )(in_vmem(place), in_vmem(block))


def solution(mesh):
    fine = Mesh(mesh.devices.reshape(ZH, ZL, X, CORE, ROW), AXES)
    col = ("zh", "zl", "x", "core")
    return jax.shard_map(
        per_device,
        mesh=fine,
        in_specs=(P(None, col, "row"), P(col, "row"), P()),
        out_specs=P(None, col, "row"),
        check_vma=False,
    )
```

```python
import jax
import jax.numpy as jnp
from jax import lax
from jax.experimental import pallas as pl
from jax.experimental.pallas import tpu as pltpu
from jax.sharding import Mesh
from jax.sharding import PartitionSpec as P

TS = 64
ZH, ZL, X, CORE, ROW = 4, 2, 4, 2, 4
TILES = ZH * ZL
AXES = ("zh", "zl", "x", "core", "row")
PIECES = 8
TARGETS = (
    (5, 0, 7, 6, 4, 1, 2, 3),
    (1, 0, 7, 2, 5, 6, 3, 4),
    (3, 2, 1, 4, 6, 7, 0, 5),
    (5, 4, 3, 2, 7, 6, 0, 1),
)
PACKED_TARGETS = tuple(sum(z << (3 * i) for i, z in enumerate(line)) for line in TARGETS)
VMEM = pl.BlockSpec(memory_space=pltpu.VMEM)
HBM = pl.BlockSpec(memory_space=pltpu.HBM)


def target_z(zh, zl, row):
    return TARGETS[zh][zl * ROW + row]


def linear(zh, zl, x, core, row):
    return (((zh * ZL + zl) * X + x) * CORE + core) * ROW + row


def delivery_pairs():
    pairs = []
    for zh in range(ZH):
        for zl in range(ZL):
            for x in range(X):
                for core in range(CORE):
                    for row in range(ROW):
                        t = target_z(zh, zl, row)
                        pairs.append((linear(zh, zl, x, core, row), linear(t // ZL, t % ZL, x, core, zh)))
    return pairs


def in_vmem(x):
    return pltpu.with_memory_space_constraint(x, pltpu.VMEM)


def in_hbm(x):
    return pltpu.with_memory_space_constraint(x, pltpu.HBM)


def lower_lanes(rows):
    return lax.broadcasted_iota(jnp.int32, (rows, 2 * TS), 1) < TS


def fetch(copies):
    for copy in copies:
        copy.start()
    for copy in copies:
        copy.wait()


def prepare_kernel(
    partner_hbm, amplitudes_hbm, sent_ref, pick_ref, odd_ref, place_ref, partner_ref, amplitudes_ref, sems
):
    fetch(
        [
            pltpu.make_async_copy(partner_hbm, partner_ref, sems.at[0]),
            pltpu.make_async_copy(amplitudes_hbm, amplitudes_ref, sems.at[1]),
        ]
    )
    zh, zl, row = lax.axis_index("zh"), lax.axis_index("zl"), lax.axis_index("row")
    for h in range(2):
        source = partner_ref[2 * row + h]
        for z in range(TILES):
            pick_ref[h, z] = jnp.full(pick_ref.shape[2:], jnp.where(source == z, 1, 0), jnp.int32)
    packed = jnp.where(zh == 0, PACKED_TARGETS[0], PACKED_TARGETS[1])
    packed = jnp.where(zh == 2, PACKED_TARGETS[2], jnp.where(zh == 3, PACKED_TARGETS[3], packed))
    target = lax.shift_right_logical(packed, 3 * (zl * ROW + row)) & (TILES - 1)
    bra = partner_ref[target]
    odd_ref[...] = jnp.full(odd_ref.shape, bra % 2, jnp.int32)
    z = zh * ZL + zl
    for h in range(2):
        place_ref[h] = jnp.full(place_ref.shape[1:], jnp.where(partner_ref[z] == 2 * row + h, 1, 0), jnp.int32)
    upper = partner_ref[z] % 2 == 1
    rows = jnp.swapaxes(amplitudes_ref[...].astype(jnp.float32), 0, 1)
    units, pairs, _ = rows.shape
    lower = lower_lanes(pairs)
    columns = []
    for j in range(units // 2):
        first, second = rows[2 * j], rows[2 * j + 1]
        from_lower = jnp.where(lower, first, pltpu.roll(second, TS, 1))
        from_upper = jnp.where(lower, pltpu.roll(first, TS, 1), second)
        columns.append(jnp.where(upper, from_upper, from_lower))
    mine = jnp.concatenate(columns, axis=1).astype(sent_ref.dtype)
    for j in range(sent_ref.shape[0]):
        sent_ref[j] = mine


def choose_kernel(pick_ref, got_ref, chosen_ref):
    tiles, pairs, width = got_ref.shape
    reps = width // pick_ref.shape[3]
    for h in range(2):
        chosen = jnp.zeros((pairs, width), jnp.float32)
        for z in range(tiles):
            wanted = jnp.concatenate([pick_ref[h, z]] * reps, axis=1) != 0
            chosen = jnp.where(wanted, got_ref[z].astype(jnp.float32), chosen)
        chosen_ref[h] = chosen.astype(chosen_ref.dtype)


def stage_top_kernel(integrals_ref, staged_ref, sems):
    step = staged_ref.shape[0] // PIECES
    parts = [pl.ds(j * step, step) for j in range(PIECES)]
    fetch([pltpu.make_async_copy(integrals_ref.at[p, :], staged_ref.at[p, :], sems.at[j]) for j, p in enumerate(parts)])


def join_kernel(first_ref, second_ref, *rest):
    out_ref = rest[-1]
    count = first_ref.shape[0]
    out_ref[pl.ds(0, count)] = first_ref[...]
    out_ref[pl.ds(count, count)] = second_ref[...]


def after_kernel(value_ref, first_ref, out_ref):
    out_ref[...] = value_ref[...]


def partial_product(packed_ref, integrals_ref, core, x):
    width = packed_ref.shape[3]
    places = [x, x + 1 - 2 * (x % 2)]
    total = jnp.zeros((packed_ref.shape[2], integrals_ref.shape[0]), jnp.float32)
    for i, place in enumerate(places):
        for h in range(2):
            start = pl.multiple_of(((h * X + place) * CORE + core) * width, width)
            total = total + lax.dot_general(
                packed_ref[i, h],
                integrals_ref[:, pl.ds(start, width)],
                (((1,), (1,)), ((), ())),
                preferred_element_type=jnp.float32,
            )
    return total


def product(packed_ref, top_ref, bottom_ref, core, x):
    return jnp.concatenate([partial_product(packed_ref, ref, core, x) for ref in (top_ref, bottom_ref)], axis=1)


def near_kernel(packed_ref, swapped_ref, top_ref, integrals_ref, bottom_ref, out_ref, sems):
    core, x = lax.axis_index("core"), lax.axis_index("x")
    rows, columns = bottom_ref.shape
    span = columns // 4
    copies = []
    for n in range(2):
        pair = (x // 2 + n) % 2
        for h in range(2):
            part = pl.ds(pl.multiple_of((2 * h + pair) * span, span), span)
            source = integrals_ref.at[pl.ds(rows, rows), part]
            copy = pltpu.make_async_copy(source, bottom_ref.at[:, part], sems.at[len(copies)])
            copy.start()
            copies.append(copy)

    def both(ref):
        return partial_product(packed_ref, ref, core, x) + partial_product(swapped_ref, ref, 1 - core, x)

    @pl.when(core >= 0)
    def _():
        out_ref[:, pl.ds(0, rows)] = both(top_ref)

    for copy in copies[:2]:
        copy.wait()

    @pl.when(x >= 0)
    def _():
        out_ref[:, pl.ds(rows, rows)] = both(bottom_ref)

    for copy in copies[2:]:
        copy.wait()


def far_kernel(packed_ref, before_ref, top_ref, bottom_ref, out_ref):
    core, x = lax.axis_index("core"), X - 1 - lax.axis_index("x")
    out_ref[...] = before_ref[...] + product(packed_ref, top_ref, bottom_ref, core, x)


def last_kernel(packed_ref, before_ref, top_ref, bottom_ref, out_ref):
    core, x = 1 - lax.axis_index("core"), X - 1 - lax.axis_index("x")
    total = before_ref[...] + product(packed_ref, top_ref, bottom_ref, core, x)
    for j in range(out_ref.shape[0]):
        out_ref[j] = total


def finish_kernel(odd_ref, shared_ref, out_ref):
    odd = jnp.concatenate([odd_ref[...]] * (out_ref.shape[1] // odd_ref.shape[1]), axis=1) != 0
    sums = []
    for h in range(2):
        total = shared_ref[h * ROW]
        for j in range(1, ROW):
            total = total + shared_ref[h * ROW + j]
        sums.append(total)
    out_ref[...] = jnp.where(odd, sums[1], sums[0]).astype(out_ref.dtype)


def place_kernel(place_ref, block_ref, out_ref):
    block = block_ref[...].astype(jnp.float32)
    pairs, width = block.shape
    lower = lower_lanes(pairs)
    left = lower & (place_ref[0] != 0)
    right = jnp.logical_not(lower) & (place_ref[1] != 0)
    rows = []
    for j in range(width // (2 * TS)):
        part = block[:, j * 2 * TS : (j + 1) * 2 * TS]
        turned = pltpu.roll(part, TS, 1)
        rows.append(jnp.where(left, part, jnp.where(right, turned, 0.0)))
        rows.append(jnp.where(left, turned, jnp.where(right, part, 0.0)))
    out_ref[...] = jnp.swapaxes(jnp.stack(rows, 0), 0, 1).astype(out_ref.dtype)


def per_device(amplitudes, integrals, partner):
    pairs, rows_dev, _ = amplitudes.shape
    width = rows_dev * TS
    bra = integrals.shape[0]
    params = pltpu.CompilerParams(vmem_limit_bytes=4 * 1024 * 1024)
    sent, pick, odd, place = pl.pallas_call(
        prepare_kernel,
        out_shape=[
            pltpu.VMEM((TILES, pairs, width), jnp.bfloat16),
            pltpu.VMEM((2, TILES, pairs, 128), jnp.int32),
            pltpu.VMEM((pairs, 128), jnp.int32),
            pltpu.VMEM((2, pairs, 128), jnp.int32),
        ],
        in_specs=[HBM, HBM],
        out_specs=[VMEM, VMEM, VMEM, VMEM],
        scratch_shapes=[
            pltpu.SMEM(partner.shape, partner.dtype),
            pltpu.VMEM(amplitudes.shape, amplitudes.dtype),
            pltpu.SemaphoreType.DMA((2,)),
        ],
        compiler_params=params,
        name="prepare",
    )(in_hbm(partner), in_hbm(amplitudes))
    got = lax.all_to_all(sent, ("zh", "zl"), 0, 0, tiled=True)
    chosen = pl.pallas_call(
        choose_kernel,
        out_shape=pltpu.VMEM((2, pairs, width), jnp.bfloat16),
        in_specs=[VMEM, VMEM],
        out_specs=VMEM,
        compiler_params=params,
        name="choose",
    )(in_vmem(pick), in_vmem(got))
    staged = pltpu.VMEM((bra // 2, integrals.shape[1]), integrals.dtype)

    def local(kernel, shape, dtype, operands, cost=None, name=None, scratch=(), specs=None):
        return pl.pallas_call(
            kernel,
            out_shape=pltpu.VMEM(shape, dtype),
            in_specs=specs or [VMEM] * len(operands),
            out_specs=VMEM,
            scratch_shapes=scratch,
            compiler_params=params,
            cost_estimate=cost,
            name=name,
        )(*operands)

    def multiply(kernel, operands, name, copies=()):
        cost = pl.CostEstimate(
            flops=pairs * integrals.size // 2, bytes_accessed=integrals.size // 2, transcendentals=0
        )
        operands = [in_vmem(operand) for operand in operands]
        return local(kernel, (*copies, pairs, bra), jnp.float32, operands, cost, name)

    core_swap = [(0, 1), (1, 0)]
    beside = lax.ppermute(chosen, "x", [(i, i ^ 1) for i in range(X)])
    top = pl.pallas_call(
        stage_top_kernel,
        out_shape=staged,
        in_specs=[HBM],
        out_specs=VMEM,
        scratch_shapes=[pltpu.SemaphoreType.DMA((PIECES,))],
        compiler_params=params,
        cost_estimate=pl.CostEstimate(flops=0, bytes_accessed=2 * integrals.size, transcendentals=0),
        name="stage_top",
    )(in_hbm(integrals))
    couple = local(
        join_kernel,
        (2, 2, pairs, width),
        chosen.dtype,
        [in_vmem(chosen[None]), in_vmem(beside[None]), in_vmem(top)],
        name="join",
    )
    swapped = lax.ppermute(couple, "core", core_swap)
    across = lax.ppermute(couple, "x", [(i, X - 1 - i) for i in range(X)])
    bottom, total = pl.pallas_call(
        near_kernel,
        out_shape=[staged, pltpu.VMEM((pairs, bra), jnp.float32)],
        in_specs=[VMEM, VMEM, VMEM, HBM],
        out_specs=[VMEM, VMEM],
        scratch_shapes=[pltpu.SemaphoreType.DMA((PIECES,))],
        compiler_params=params,
        cost_estimate=pl.CostEstimate(
            flops=pairs * integrals.size, bytes_accessed=2 * integrals.size, transcendentals=0
        ),
        name="near_product",
    )(in_vmem(couple), in_vmem(swapped), in_vmem(top), in_hbm(integrals))
    across = local(after_kernel, across.shape, across.dtype, [in_vmem(across), in_vmem(total)], name="after")
    swapped = lax.ppermute(across, "core", core_swap)
    total = multiply(far_kernel, [across, total, top, bottom], "far_product")
    partials = multiply(last_kernel, [swapped, total, top, bottom], "last_product", (ZL * ROW,))
    shared = lax.all_to_all(partials, ("zl", "row"), 0, 0, tiled=True)
    block = pl.pallas_call(
        finish_kernel,
        out_shape=pltpu.VMEM((pairs, bra), jnp.bfloat16),
        in_specs=[VMEM, VMEM],
        out_specs=VMEM,
        compiler_params=params,
        name="finish",
    )(in_vmem(odd), in_vmem(shared))
    block = lax.ppermute(block, AXES, delivery_pairs())
    return pl.pallas_call(
        place_kernel,
        out_shape=jax.ShapeDtypeStruct(amplitudes.shape, jnp.bfloat16),
        in_specs=[VMEM, VMEM],
        out_specs=VMEM,
        compiler_params=params,
        name="place",
    )(in_vmem(place), in_vmem(block))


def solution(mesh):
    fine = Mesh(mesh.devices.reshape(ZH, ZL, X, CORE, ROW), AXES)
    col = ("zh", "zl", "x", "core")
    return jax.shard_map(
        per_device,
        mesh=fine,
        in_specs=(P(None, col, "row"), P(col, "row"), P()),
        out_specs=P(None, col, "row"),
        check_vma=False,
    )
```

```python
import jax
import jax.numpy as jnp
from jax import lax
from jax.experimental import pallas as pl
from jax.experimental.pallas import tpu as pltpu
from jax.sharding import Mesh
from jax.sharding import PartitionSpec as P

TS = 64
ZH, ZL, X, CORE, ROW = 4, 2, 4, 2, 4
TILES = ZH * ZL
AXES = ("zh", "zl", "x", "core", "row")
PIECES = 8
Z_ORDER = (5, 6, 7, 0, 1, 2, 3, 4)
GROUP_ORDER = (2, 6, 3, 7, 0, 4, 1, 5)
TARGETS = (
    (5, 0, 7, 6, 4, 1, 2, 3),
    (1, 0, 7, 2, 5, 6, 3, 4),
    (3, 2, 1, 4, 6, 7, 0, 5),
    (5, 4, 3, 2, 7, 6, 0, 1),
)
PACKED_TARGETS = tuple(sum(z << (3 * i) for i, z in enumerate(line)) for line in TARGETS)
VMEM = pl.BlockSpec(memory_space=pltpu.VMEM)
HBM = pl.BlockSpec(memory_space=pltpu.HBM)


def target_z(zh, zl, row):
    return TARGETS[zh][zl * ROW + row]


def linear(zh, zl, x, core, row):
    return (((zh * ZL + zl) * X + x) * CORE + core) * ROW + row


def delivery_pairs():
    pairs = []
    for zh in range(ZH):
        for zl in range(ZL):
            for x in range(X):
                for core in range(CORE):
                    for row in range(ROW):
                        t = target_z(zh, zl, row)
                        pairs.append((linear(zh, zl, x, core, row), linear(t // ZL, t % ZL, x, core, zh)))
    return pairs


def in_vmem(x):
    return pltpu.with_memory_space_constraint(x, pltpu.VMEM)


def in_hbm(x):
    return pltpu.with_memory_space_constraint(x, pltpu.HBM)


def lower_lanes(rows):
    return lax.broadcasted_iota(jnp.int32, (rows, 2 * TS), 1) < TS


def fetch(copies):
    for copy in copies:
        copy.start()
    for copy in copies:
        copy.wait()


def prepare_kernel(
    partner_hbm, amplitudes_hbm, sent_ref, pick_ref, odd_ref, place_ref, partner_ref, amplitudes_ref, sems
):
    fetch(
        [
            pltpu.make_async_copy(partner_hbm, partner_ref, sems.at[0]),
            pltpu.make_async_copy(amplitudes_hbm, amplitudes_ref, sems.at[1]),
        ]
    )
    zh, zl, row = lax.axis_index("zh"), lax.axis_index("zl"), lax.axis_index("row")
    for h in range(2):
        source = partner_ref[2 * row + h]
        for place, z in enumerate(Z_ORDER):
            pick_ref[h, place] = jnp.full(pick_ref.shape[2:], jnp.where(source == z, 1, 0), jnp.int32)
    packed = jnp.where(zh == 0, PACKED_TARGETS[0], PACKED_TARGETS[1])
    packed = jnp.where(zh == 2, PACKED_TARGETS[2], jnp.where(zh == 3, PACKED_TARGETS[3], packed))
    target = lax.shift_right_logical(packed, 3 * (zl * ROW + row)) & (TILES - 1)
    bra = partner_ref[target]
    odd_ref[...] = jnp.full(odd_ref.shape, bra % 2, jnp.int32)
    z = zh * ZL + zl
    for h in range(2):
        place_ref[h] = jnp.full(place_ref.shape[1:], jnp.where(partner_ref[z] == 2 * row + h, 1, 0), jnp.int32)
    upper = partner_ref[z] % 2 == 1
    rows = jnp.swapaxes(amplitudes_ref[...].astype(jnp.float32), 0, 1)
    units, pairs, _ = rows.shape
    lower = lower_lanes(pairs)
    columns = []
    for j in range(units // 2):
        first, second = rows[2 * j], rows[2 * j + 1]
        from_lower = jnp.where(lower, first, pltpu.roll(second, TS, 1))
        from_upper = jnp.where(lower, pltpu.roll(first, TS, 1), second)
        columns.append(jnp.where(upper, from_upper, from_lower))
    mine = jnp.concatenate(columns, axis=1).astype(sent_ref.dtype)
    for j in range(sent_ref.shape[0]):
        sent_ref[j] = mine


def choose_kernel(pick_ref, got_ref, chosen_ref):
    tiles, pairs, width = got_ref.shape
    reps = width // pick_ref.shape[3]
    for h in range(2):
        chosen = jnp.zeros((pairs, width), jnp.float32)
        for z in range(tiles):
            wanted = jnp.concatenate([pick_ref[h, z]] * reps, axis=1) != 0
            chosen = jnp.where(wanted, got_ref[z].astype(jnp.float32), chosen)
        chosen_ref[h] = chosen.astype(chosen_ref.dtype)


def stage_top_kernel(integrals_ref, staged_ref, sems):
    step = staged_ref.shape[0] // PIECES
    parts = [pl.ds(j * step, step) for j in range(PIECES)]
    fetch([pltpu.make_async_copy(integrals_ref.at[p, :], staged_ref.at[p, :], sems.at[j]) for j, p in enumerate(parts)])


def join_kernel(first_ref, second_ref, *rest):
    out_ref = rest[-1]
    count = first_ref.shape[0]
    out_ref[pl.ds(0, count)] = first_ref[...]
    out_ref[pl.ds(count, count)] = second_ref[...]


def after_kernel(value_ref, first_ref, out_ref):
    out_ref[...] = value_ref[...]


def partial_product(packed_ref, integrals_ref, core, x):
    width = packed_ref.shape[3]
    places = [x, x + 1 - 2 * (x % 2)]
    total = jnp.zeros((packed_ref.shape[2], integrals_ref.shape[0]), jnp.float32)
    for i, place in enumerate(places):
        for h in range(2):
            start = pl.multiple_of(((h * X + place) * CORE + core) * width, width)
            total = total + lax.dot_general(
                packed_ref[i, h],
                integrals_ref[:, pl.ds(start, width)],
                (((1,), (1,)), ((), ())),
                preferred_element_type=jnp.float32,
            )
    return total


def product(packed_ref, top_ref, bottom_ref, core, x):
    return jnp.concatenate([partial_product(packed_ref, ref, core, x) for ref in (top_ref, bottom_ref)], axis=1)


def near_kernel(packed_ref, swapped_ref, top_ref, integrals_ref, bottom_ref, out_ref, sems):
    core, x = lax.axis_index("core"), lax.axis_index("x")
    rows, columns = bottom_ref.shape
    span = columns // 4
    copies = []
    for n in range(2):
        pair = (x // 2 + n) % 2
        for h in range(2):
            part = pl.ds(pl.multiple_of((2 * h + pair) * span, span), span)
            source = integrals_ref.at[pl.ds(rows, rows), part]
            copy = pltpu.make_async_copy(source, bottom_ref.at[:, part], sems.at[len(copies)])
            copy.start()
            copies.append(copy)

    def both(ref):
        return partial_product(packed_ref, ref, core, x) + partial_product(swapped_ref, ref, 1 - core, x)

    @pl.when(core >= 0)
    def _():
        out_ref[:, pl.ds(0, rows)] = both(top_ref)

    for copy in copies[:2]:
        copy.wait()

    @pl.when(x >= 0)
    def _():
        out_ref[:, pl.ds(rows, rows)] = both(bottom_ref)

    for copy in copies[2:]:
        copy.wait()


def far_kernel(packed_ref, before_ref, top_ref, bottom_ref, out_ref):
    core, x = lax.axis_index("core"), X - 1 - lax.axis_index("x")
    out_ref[...] = before_ref[...] + product(packed_ref, top_ref, bottom_ref, core, x)


def last_kernel(packed_ref, before_ref, top_ref, bottom_ref, out_ref):
    core, x = 1 - lax.axis_index("core"), X - 1 - lax.axis_index("x")
    total = before_ref[...] + product(packed_ref, top_ref, bottom_ref, core, x)
    for j in range(out_ref.shape[0]):
        out_ref[j] = total


def finish_kernel(odd_ref, shared_ref, out_ref):
    odd = jnp.concatenate([odd_ref[...]] * (out_ref.shape[1] // odd_ref.shape[1]), axis=1) != 0
    sums = []
    for h in range(2):
        total = shared_ref[GROUP_ORDER.index(h * ROW)]
        for j in range(1, ROW):
            total = total + shared_ref[GROUP_ORDER.index(h * ROW + j)]
        sums.append(total)
    out_ref[...] = jnp.where(odd, sums[1], sums[0]).astype(out_ref.dtype)


def place_kernel(place_ref, block_ref, out_ref):
    block = block_ref[...].astype(jnp.float32)
    pairs, width = block.shape
    lower = lower_lanes(pairs)
    left = lower & (place_ref[0] != 0)
    right = jnp.logical_not(lower) & (place_ref[1] != 0)
    rows = []
    for j in range(width // (2 * TS)):
        part = block[:, j * 2 * TS : (j + 1) * 2 * TS]
        turned = pltpu.roll(part, TS, 1)
        rows.append(jnp.where(left, part, jnp.where(right, turned, 0.0)))
        rows.append(jnp.where(left, turned, jnp.where(right, part, 0.0)))
    out_ref[...] = jnp.swapaxes(jnp.stack(rows, 0), 0, 1).astype(out_ref.dtype)


def per_device(amplitudes, integrals, partner):
    pairs, rows_dev, _ = amplitudes.shape
    width = rows_dev * TS
    bra = integrals.shape[0]
    params = pltpu.CompilerParams(vmem_limit_bytes=4 * 1024 * 1024)
    sent, pick, odd, place = pl.pallas_call(
        prepare_kernel,
        out_shape=[
            pltpu.VMEM((TILES, pairs, width), jnp.bfloat16),
            pltpu.VMEM((2, TILES, pairs, 128), jnp.int32),
            pltpu.VMEM((pairs, 128), jnp.int32),
            pltpu.VMEM((2, pairs, 128), jnp.int32),
        ],
        in_specs=[HBM, HBM],
        out_specs=[VMEM, VMEM, VMEM, VMEM],
        scratch_shapes=[
            pltpu.SMEM(partner.shape, partner.dtype),
            pltpu.VMEM(amplitudes.shape, amplitudes.dtype),
            pltpu.SemaphoreType.DMA((2,)),
        ],
        compiler_params=params,
        name="prepare",
    )(in_hbm(partner), in_hbm(amplitudes))
    got = lax.all_to_all(sent, ("zh", "zl"), 0, 0, axis_index_groups=[list(Z_ORDER)], tiled=True)
    chosen = pl.pallas_call(
        choose_kernel,
        out_shape=pltpu.VMEM((2, pairs, width), jnp.bfloat16),
        in_specs=[VMEM, VMEM],
        out_specs=VMEM,
        compiler_params=params,
        name="choose",
    )(in_vmem(pick), in_vmem(got))
    staged = pltpu.VMEM((bra // 2, integrals.shape[1]), integrals.dtype)

    def local(kernel, shape, dtype, operands, cost=None, name=None, scratch=(), specs=None):
        return pl.pallas_call(
            kernel,
            out_shape=pltpu.VMEM(shape, dtype),
            in_specs=specs or [VMEM] * len(operands),
            out_specs=VMEM,
            scratch_shapes=scratch,
            compiler_params=params,
            cost_estimate=cost,
            name=name,
        )(*operands)

    def multiply(kernel, operands, name, copies=()):
        cost = pl.CostEstimate(
            flops=pairs * integrals.size // 2, bytes_accessed=integrals.size // 2, transcendentals=0
        )
        operands = [in_vmem(operand) for operand in operands]
        return local(kernel, (*copies, pairs, bra), jnp.float32, operands, cost, name)

    core_swap = [(0, 1), (1, 0)]
    beside = lax.ppermute(chosen, "x", [(i, i ^ 1) for i in range(X)])
    top = pl.pallas_call(
        stage_top_kernel,
        out_shape=staged,
        in_specs=[HBM],
        out_specs=VMEM,
        scratch_shapes=[pltpu.SemaphoreType.DMA((PIECES,))],
        compiler_params=params,
        cost_estimate=pl.CostEstimate(flops=0, bytes_accessed=2 * integrals.size, transcendentals=0),
        name="stage_top",
    )(in_hbm(integrals))
    couple = local(
        join_kernel,
        (2, 2, pairs, width),
        chosen.dtype,
        [in_vmem(chosen[None]), in_vmem(beside[None]), in_vmem(top)],
        name="join",
    )
    swapped = lax.ppermute(couple, "core", core_swap)
    across = lax.ppermute(couple, "x", [(i, X - 1 - i) for i in range(X)])
    bottom, total = pl.pallas_call(
        near_kernel,
        out_shape=[staged, pltpu.VMEM((pairs, bra), jnp.float32)],
        in_specs=[VMEM, VMEM, VMEM, HBM],
        out_specs=[VMEM, VMEM],
        scratch_shapes=[pltpu.SemaphoreType.DMA((PIECES,))],
        compiler_params=params,
        cost_estimate=pl.CostEstimate(
            flops=pairs * integrals.size, bytes_accessed=2 * integrals.size, transcendentals=0
        ),
        name="near_product",
    )(in_vmem(couple), in_vmem(swapped), in_vmem(top), in_hbm(integrals))
    across = local(after_kernel, across.shape, across.dtype, [in_vmem(across), in_vmem(total)], name="after")
    swapped = lax.ppermute(across, "core", core_swap)
    total = multiply(far_kernel, [across, total, top, bottom], "far_product")
    partials = multiply(last_kernel, [swapped, total, top, bottom], "last_product", (ZL * ROW,))
    shared = lax.all_to_all(partials, ("zl", "row"), 0, 0, axis_index_groups=[list(GROUP_ORDER)], tiled=True)
    block = pl.pallas_call(
        finish_kernel,
        out_shape=pltpu.VMEM((pairs, bra), jnp.bfloat16),
        in_specs=[VMEM, VMEM],
        out_specs=VMEM,
        compiler_params=params,
        name="finish",
    )(in_vmem(odd), in_vmem(shared))
    block = lax.ppermute(block, AXES, delivery_pairs())
    return pl.pallas_call(
        place_kernel,
        out_shape=jax.ShapeDtypeStruct(amplitudes.shape, jnp.bfloat16),
        in_specs=[VMEM, VMEM],
        out_specs=VMEM,
        compiler_params=params,
        name="place",
    )(in_vmem(place), in_vmem(block))


def solution(mesh):
    fine = Mesh(mesh.devices.reshape(ZH, ZL, X, CORE, ROW), AXES)
    col = ("zh", "zl", "x", "core")
    return jax.shard_map(
        per_device,
        mesh=fine,
        in_specs=(P(None, col, "row"), P(col, "row"), P()),
        out_specs=P(None, col, "row"),
        check_vma=False,
    )
```

```python
import jax
import jax.numpy as jnp
from jax import lax
from jax.experimental import pallas as pl
from jax.experimental.pallas import tpu as pltpu
from jax.sharding import Mesh
from jax.sharding import PartitionSpec as P

TS = 64
ZH, ZL, X, CORE, ROW = 4, 2, 4, 2, 4
TILES = ZH * ZL
AXES = ("zh", "zl", "x", "core", "row")
PIECES = 8
Z_ORDER = (5, 4, 6, 7, 0, 1, 2, 3)
GROUP_ORDER = (2, 6, 3, 7, 0, 4, 1, 5)
TARGETS = (
    (5, 0, 7, 6, 4, 1, 2, 3),
    (1, 0, 7, 2, 5, 6, 3, 4),
    (3, 2, 1, 4, 6, 7, 0, 5),
    (5, 4, 3, 2, 7, 6, 0, 1),
)
PACKED_TARGETS = tuple(sum(z << (3 * i) for i, z in enumerate(line)) for line in TARGETS)
VMEM = pl.BlockSpec(memory_space=pltpu.VMEM)
HBM = pl.BlockSpec(memory_space=pltpu.HBM)


def target_z(zh, zl, row):
    return TARGETS[zh][zl * ROW + row]


def linear(zh, zl, x, core, row):
    return (((zh * ZL + zl) * X + x) * CORE + core) * ROW + row


def delivery_pairs():
    pairs = []
    for zh in range(ZH):
        for zl in range(ZL):
            for x in range(X):
                for core in range(CORE):
                    for row in range(ROW):
                        t = target_z(zh, zl, row)
                        pairs.append((linear(zh, zl, x, core, row), linear(t // ZL, t % ZL, x, core, zh)))
    return pairs


def in_vmem(x):
    return pltpu.with_memory_space_constraint(x, pltpu.VMEM)


def in_hbm(x):
    return pltpu.with_memory_space_constraint(x, pltpu.HBM)


def lower_lanes(rows):
    return lax.broadcasted_iota(jnp.int32, (rows, 2 * TS), 1) < TS


def fetch(copies):
    for copy in copies:
        copy.start()
    for copy in copies:
        copy.wait()


def prepare_kernel(
    partner_hbm, amplitudes_hbm, sent_ref, pick_ref, odd_ref, place_ref, partner_ref, amplitudes_ref, sems
):
    fetch(
        [
            pltpu.make_async_copy(partner_hbm, partner_ref, sems.at[0]),
            pltpu.make_async_copy(amplitudes_hbm, amplitudes_ref, sems.at[1]),
        ]
    )
    zh, zl, row = lax.axis_index("zh"), lax.axis_index("zl"), lax.axis_index("row")
    for h in range(2):
        source = partner_ref[2 * row + h]
        for place, z in enumerate(Z_ORDER):
            pick_ref[h, place] = jnp.full(pick_ref.shape[2:], jnp.where(source == z, 1, 0), jnp.int32)
    packed = jnp.where(zh == 0, PACKED_TARGETS[0], PACKED_TARGETS[1])
    packed = jnp.where(zh == 2, PACKED_TARGETS[2], jnp.where(zh == 3, PACKED_TARGETS[3], packed))
    target = lax.shift_right_logical(packed, 3 * (zl * ROW + row)) & (TILES - 1)
    bra = partner_ref[target]
    odd_ref[...] = jnp.full(odd_ref.shape, bra % 2, jnp.int32)
    z = zh * ZL + zl
    for h in range(2):
        place_ref[h] = jnp.full(place_ref.shape[1:], jnp.where(partner_ref[z] == 2 * row + h, 1, 0), jnp.int32)
    upper = partner_ref[z] % 2 == 1
    rows = jnp.swapaxes(amplitudes_ref[...].astype(jnp.float32), 0, 1)
    units, pairs, _ = rows.shape
    lower = lower_lanes(pairs)
    columns = []
    for j in range(units // 2):
        first, second = rows[2 * j], rows[2 * j + 1]
        from_lower = jnp.where(lower, first, pltpu.roll(second, TS, 1))
        from_upper = jnp.where(lower, pltpu.roll(first, TS, 1), second)
        columns.append(jnp.where(upper, from_upper, from_lower))
    mine = jnp.concatenate(columns, axis=1).astype(sent_ref.dtype)
    for j in range(sent_ref.shape[0]):
        sent_ref[j] = mine


def choose_kernel(pick_ref, got_ref, chosen_ref):
    tiles, pairs, width = got_ref.shape
    reps = width // pick_ref.shape[3]
    for h in range(2):
        chosen = jnp.zeros((pairs, width), jnp.float32)
        for z in range(tiles):
            wanted = jnp.concatenate([pick_ref[h, z]] * reps, axis=1) != 0
            chosen = jnp.where(wanted, got_ref[z].astype(jnp.float32), chosen)
        chosen_ref[h] = chosen.astype(chosen_ref.dtype)


def stage_top_kernel(integrals_ref, staged_ref, sems):
    step = staged_ref.shape[0] // PIECES
    parts = [pl.ds(j * step, step) for j in range(PIECES)]
    fetch([pltpu.make_async_copy(integrals_ref.at[p, :], staged_ref.at[p, :], sems.at[j]) for j, p in enumerate(parts)])


def join_kernel(first_ref, second_ref, *rest):
    out_ref = rest[-1]
    count = first_ref.shape[0]
    out_ref[pl.ds(0, count)] = first_ref[...]
    out_ref[pl.ds(count, count)] = second_ref[...]


def after_kernel(value_ref, first_ref, out_ref):
    out_ref[...] = value_ref[...]


def facing(x):
    return X - 1 - x


def beside(x):
    return x + 1 - 2 * (x % 2)


def partial_product(packed_ref, integrals_ref, core, x):
    width = packed_ref.shape[3]
    places = [x, facing(x)]
    total = jnp.zeros((packed_ref.shape[2], integrals_ref.shape[0]), jnp.float32)
    for i, place in enumerate(places):
        for h in range(2):
            start = pl.multiple_of(((h * X + place) * CORE + core) * width, width)
            total = total + lax.dot_general(
                packed_ref[i, h],
                integrals_ref[:, pl.ds(start, width)],
                (((1,), (1,)), ((), ())),
                preferred_element_type=jnp.float32,
            )
    return total


def product(packed_ref, top_ref, bottom_ref, core, x):
    return jnp.concatenate([partial_product(packed_ref, ref, core, x) for ref in (top_ref, bottom_ref)], axis=1)


def near_kernel(packed_ref, swapped_ref, top_ref, integrals_ref, bottom_ref, out_ref, sems):
    core, x = lax.axis_index("core"), lax.axis_index("x")
    rows, columns = bottom_ref.shape
    span = columns // (2 * X)
    copies = []
    for place in (x, facing(x), beside(x), facing(beside(x))):
        for h in range(2):
            part = pl.ds(pl.multiple_of((h * X + place) * span, span), span)
            source = integrals_ref.at[pl.ds(rows, rows), part]
            copy = pltpu.make_async_copy(source, bottom_ref.at[:, part], sems.at[len(copies)])
            copy.start()
            copies.append(copy)

    def both(ref):
        return partial_product(packed_ref, ref, core, x) + partial_product(swapped_ref, ref, 1 - core, x)

    @pl.when(core >= 0)
    def _():
        out_ref[:, pl.ds(0, rows)] = both(top_ref)

    for copy in copies[:4]:
        copy.wait()

    @pl.when(x >= 0)
    def _():
        out_ref[:, pl.ds(rows, rows)] = both(bottom_ref)

    for copy in copies[4:]:
        copy.wait()


def far_kernel(packed_ref, before_ref, top_ref, bottom_ref, out_ref):
    core, x = lax.axis_index("core"), beside(lax.axis_index("x"))
    out_ref[...] = before_ref[...] + product(packed_ref, top_ref, bottom_ref, core, x)


def last_kernel(packed_ref, before_ref, top_ref, bottom_ref, out_ref):
    core, x = 1 - lax.axis_index("core"), beside(lax.axis_index("x"))
    total = before_ref[...] + product(packed_ref, top_ref, bottom_ref, core, x)
    for j in range(out_ref.shape[0]):
        out_ref[j] = total


def finish_kernel(odd_ref, shared_ref, out_ref):
    odd = jnp.concatenate([odd_ref[...]] * (out_ref.shape[1] // odd_ref.shape[1]), axis=1) != 0
    sums = []
    for h in range(2):
        total = shared_ref[GROUP_ORDER.index(h * ROW)]
        for j in range(1, ROW):
            total = total + shared_ref[GROUP_ORDER.index(h * ROW + j)]
        sums.append(total)
    out_ref[...] = jnp.where(odd, sums[1], sums[0]).astype(out_ref.dtype)


def place_kernel(place_ref, block_ref, out_ref):
    block = block_ref[...].astype(jnp.float32)
    pairs, width = block.shape
    lower = lower_lanes(pairs)
    left = lower & (place_ref[0] != 0)
    right = jnp.logical_not(lower) & (place_ref[1] != 0)
    rows = []
    for j in range(width // (2 * TS)):
        part = block[:, j * 2 * TS : (j + 1) * 2 * TS]
        turned = pltpu.roll(part, TS, 1)
        rows.append(jnp.where(left, part, jnp.where(right, turned, 0.0)))
        rows.append(jnp.where(left, turned, jnp.where(right, part, 0.0)))
    out_ref[...] = jnp.swapaxes(jnp.stack(rows, 0), 0, 1).astype(out_ref.dtype)


def per_device(amplitudes, integrals, partner):
    pairs, rows_dev, _ = amplitudes.shape
    width = rows_dev * TS
    bra = integrals.shape[0]
    params = pltpu.CompilerParams(vmem_limit_bytes=4 * 1024 * 1024)
    sent, pick, odd, place = pl.pallas_call(
        prepare_kernel,
        out_shape=[
            pltpu.VMEM((TILES, pairs, width), jnp.bfloat16),
            pltpu.VMEM((2, TILES, pairs, 128), jnp.int32),
            pltpu.VMEM((pairs, 128), jnp.int32),
            pltpu.VMEM((2, pairs, 128), jnp.int32),
        ],
        in_specs=[HBM, HBM],
        out_specs=[VMEM, VMEM, VMEM, VMEM],
        scratch_shapes=[
            pltpu.SMEM(partner.shape, partner.dtype),
            pltpu.VMEM(amplitudes.shape, amplitudes.dtype),
            pltpu.SemaphoreType.DMA((2,)),
        ],
        compiler_params=params,
        name="prepare",
    )(in_hbm(partner), in_hbm(amplitudes))
    got = lax.all_to_all(sent, ("zh", "zl"), 0, 0, axis_index_groups=[list(Z_ORDER)], tiled=True)
    chosen = pl.pallas_call(
        choose_kernel,
        out_shape=pltpu.VMEM((2, pairs, width), jnp.bfloat16),
        in_specs=[VMEM, VMEM],
        out_specs=VMEM,
        compiler_params=params,
        name="choose",
    )(in_vmem(pick), in_vmem(got))
    staged = pltpu.VMEM((bra // 2, integrals.shape[1]), integrals.dtype)

    def local(kernel, shape, dtype, operands, cost=None, name=None, scratch=(), specs=None):
        return pl.pallas_call(
            kernel,
            out_shape=pltpu.VMEM(shape, dtype),
            in_specs=specs or [VMEM] * len(operands),
            out_specs=VMEM,
            scratch_shapes=scratch,
            compiler_params=params,
            cost_estimate=cost,
            name=name,
        )(*operands)

    def multiply(kernel, operands, name, copies=()):
        cost = pl.CostEstimate(
            flops=pairs * integrals.size // 2, bytes_accessed=integrals.size // 2, transcendentals=0
        )
        operands = [in_vmem(operand) for operand in operands]
        return local(kernel, (*copies, pairs, bra), jnp.float32, operands, cost, name)

    core_swap = [(0, 1), (1, 0)]
    opposite = lax.ppermute(chosen, "x", [(i, facing(i)) for i in range(X)])
    top = pl.pallas_call(
        stage_top_kernel,
        out_shape=staged,
        in_specs=[HBM],
        out_specs=VMEM,
        scratch_shapes=[pltpu.SemaphoreType.DMA((PIECES,))],
        compiler_params=params,
        cost_estimate=pl.CostEstimate(flops=0, bytes_accessed=2 * integrals.size, transcendentals=0),
        name="stage_top",
    )(in_hbm(integrals))
    couple = local(
        join_kernel,
        (2, 2, pairs, width),
        chosen.dtype,
        [in_vmem(chosen[None]), in_vmem(opposite[None]), in_vmem(top)],
        name="join",
    )
    swapped = lax.ppermute(couple, "core", core_swap)
    across = lax.ppermute(couple, "x", [(i, beside(i)) for i in range(X)])
    bottom, total = pl.pallas_call(
        near_kernel,
        out_shape=[staged, pltpu.VMEM((pairs, bra), jnp.float32)],
        in_specs=[VMEM, VMEM, VMEM, HBM],
        out_specs=[VMEM, VMEM],
        scratch_shapes=[pltpu.SemaphoreType.DMA((PIECES,))],
        compiler_params=params,
        cost_estimate=pl.CostEstimate(
            flops=pairs * integrals.size, bytes_accessed=2 * integrals.size, transcendentals=0
        ),
        name="near_product",
    )(in_vmem(couple), in_vmem(swapped), in_vmem(top), in_hbm(integrals))
    across = local(after_kernel, across.shape, across.dtype, [in_vmem(across), in_vmem(total)], name="after")
    swapped = lax.ppermute(across, "core", core_swap)
    total = multiply(far_kernel, [across, total, top, bottom], "far_product")
    partials = multiply(last_kernel, [swapped, total, top, bottom], "last_product", (ZL * ROW,))
    shared = lax.all_to_all(partials, ("zl", "row"), 0, 0, axis_index_groups=[list(GROUP_ORDER)], tiled=True)
    block = pl.pallas_call(
        finish_kernel,
        out_shape=pltpu.VMEM((pairs, bra), jnp.bfloat16),
        in_specs=[VMEM, VMEM],
        out_specs=VMEM,
        compiler_params=params,
        name="finish",
    )(in_vmem(odd), in_vmem(shared))
    block = lax.ppermute(block, AXES, delivery_pairs())
    return pl.pallas_call(
        place_kernel,
        out_shape=jax.ShapeDtypeStruct(amplitudes.shape, jnp.bfloat16),
        in_specs=[VMEM, VMEM],
        out_specs=VMEM,
        compiler_params=params,
        name="place",
    )(in_vmem(place), in_vmem(block))


def solution(mesh):
    fine = Mesh(mesh.devices.reshape(ZH, ZL, X, CORE, ROW), AXES)
    col = ("zh", "zl", "x", "core")
    return jax.shard_map(
        per_device,
        mesh=fine,
        in_specs=(P(None, col, "row"), P(col, "row"), P()),
        out_specs=P(None, col, "row"),
        check_vma=False,
    )
```

```python
import jax
import jax.numpy as jnp
from jax import lax
from jax.experimental import pallas as pl
from jax.experimental.pallas import tpu as pltpu
from jax.sharding import Mesh
from jax.sharding import PartitionSpec as P

TS = 64
ZH, ZL, X, CORE, ROW = 4, 2, 4, 2, 4
TILES = ZH * ZL
AXES = ("zh", "zl", "x", "core", "row")
PIECES = 8
Z_ORDER = (5, 4, 6, 7, 0, 1, 2, 3)
GROUP_ORDER = (2, 6, 3, 7, 0, 4, 1, 5)
TARGETS = (
    (5, 0, 7, 6, 4, 1, 2, 3),
    (1, 0, 7, 2, 5, 6, 3, 4),
    (3, 2, 1, 4, 6, 7, 0, 5),
    (5, 4, 3, 2, 7, 6, 0, 1),
)
PACKED_TARGETS = tuple(sum(z << (3 * i) for i, z in enumerate(line)) for line in TARGETS)
VMEM = pl.BlockSpec(memory_space=pltpu.VMEM)
HBM = pl.BlockSpec(memory_space=pltpu.HBM)


def target_z(zh, zl, row):
    return TARGETS[zh][zl * ROW + row]


def linear(zh, zl, x, core, row):
    return (((zh * ZL + zl) * X + x) * CORE + core) * ROW + row


def delivery_pairs():
    pairs = []
    for zh in range(ZH):
        for zl in range(ZL):
            for x in range(X):
                for core in range(CORE):
                    for row in range(ROW):
                        t = target_z(zh, zl, row)
                        pairs.append((linear(zh, zl, x, core, row), linear(t // ZL, t % ZL, x, core, zh)))
    return pairs


def in_vmem(x):
    return pltpu.with_memory_space_constraint(x, pltpu.VMEM)


def in_hbm(x):
    return pltpu.with_memory_space_constraint(x, pltpu.HBM)


def lower_lanes(rows):
    return lax.broadcasted_iota(jnp.int32, (rows, 2 * TS), 1) < TS


def fetch(copies):
    for copy in copies:
        copy.start()
    for copy in copies:
        copy.wait()


def prepare_kernel(
    partner_hbm, amplitudes_hbm, sent_ref, pick_ref, odd_ref, place_ref, partner_ref, amplitudes_ref, sems
):
    copies = [
        pltpu.make_async_copy(partner_hbm, partner_ref, sems.at[0]),
        pltpu.make_async_copy(amplitudes_hbm, amplitudes_ref, sems.at[1]),
    ]
    for copy in copies:
        copy.start()
    copies[0].wait()
    zh, zl, row = lax.axis_index("zh"), lax.axis_index("zl"), lax.axis_index("row")
    for h in range(2):
        source = partner_ref[2 * row + h]
        for place, z in enumerate(Z_ORDER):
            pick_ref[h, place] = jnp.full(pick_ref.shape[2:], jnp.where(source == z, 1, 0), jnp.int32)
    packed = jnp.where(zh == 0, PACKED_TARGETS[0], PACKED_TARGETS[1])
    packed = jnp.where(zh == 2, PACKED_TARGETS[2], jnp.where(zh == 3, PACKED_TARGETS[3], packed))
    target = lax.shift_right_logical(packed, 3 * (zl * ROW + row)) & (TILES - 1)
    bra = partner_ref[target]
    odd_ref[...] = jnp.full(odd_ref.shape, bra % 2, jnp.int32)
    z = zh * ZL + zl
    for h in range(2):
        place_ref[h] = jnp.full(place_ref.shape[1:], jnp.where(partner_ref[z] == 2 * row + h, 1, 0), jnp.int32)
    upper = partner_ref[z] % 2 == 1
    copies[1].wait()
    rows = jnp.swapaxes(amplitudes_ref[...].astype(jnp.float32), 0, 1)
    units, pairs, _ = rows.shape
    lower = lower_lanes(pairs)
    columns = []
    for j in range(units // 2):
        first, second = rows[2 * j], rows[2 * j + 1]
        from_lower = jnp.where(lower, first, pltpu.roll(second, TS, 1))
        from_upper = jnp.where(lower, pltpu.roll(first, TS, 1), second)
        columns.append(jnp.where(upper, from_upper, from_lower))
    mine = jnp.concatenate(columns, axis=1).astype(sent_ref.dtype)
    for j in range(sent_ref.shape[0]):
        sent_ref[j] = mine


def choose_kernel(pick_ref, got_ref, chosen_ref):
    tiles, pairs, width = got_ref.shape
    reps = width // pick_ref.shape[3]
    for h in range(2):
        chosen = jnp.zeros((pairs, width), jnp.float32)
        for z in range(tiles):
            wanted = jnp.concatenate([pick_ref[h, z]] * reps, axis=1) != 0
            chosen = jnp.where(wanted, got_ref[z].astype(jnp.float32), chosen)
        chosen_ref[h] = chosen.astype(chosen_ref.dtype)


def stage_top_kernel(integrals_ref, staged_ref, sems):
    step = staged_ref.shape[0] // PIECES
    parts = [pl.ds(j * step, step) for j in range(PIECES)]
    fetch([pltpu.make_async_copy(integrals_ref.at[p, :], staged_ref.at[p, :], sems.at[j]) for j, p in enumerate(parts)])


def join_kernel(first_ref, second_ref, *rest):
    out_ref = rest[-1]
    count = first_ref.shape[0]
    out_ref[pl.ds(0, count)] = first_ref[...]
    out_ref[pl.ds(count, count)] = second_ref[...]


def after_kernel(value_ref, first_ref, out_ref):
    out_ref[...] = value_ref[...]


def partial_product(packed_ref, integrals_ref, core, x):
    width = packed_ref.shape[3]
    places = [x, x + 1 - 2 * (x % 2)]
    total = jnp.zeros((packed_ref.shape[2], integrals_ref.shape[0]), jnp.float32)
    for i, place in enumerate(places):
        for h in range(2):
            start = pl.multiple_of(((h * X + place) * CORE + core) * width, width)
            total = total + lax.dot_general(
                packed_ref[i, h],
                integrals_ref[:, pl.ds(start, width)],
                (((1,), (1,)), ((), ())),
                preferred_element_type=jnp.float32,
            )
    return total


def product(packed_ref, top_ref, bottom_ref, core, x):
    return jnp.concatenate([partial_product(packed_ref, ref, core, x) for ref in (top_ref, bottom_ref)], axis=1)


def near_kernel(packed_ref, swapped_ref, top_ref, integrals_ref, bottom_ref, out_ref, sems):
    core, x = lax.axis_index("core"), lax.axis_index("x")
    rows, columns = bottom_ref.shape
    span = columns // 4
    copies = []
    for n in range(2):
        pair = (x // 2 + n) % 2
        for h in range(2):
            part = pl.ds(pl.multiple_of((2 * h + pair) * span, span), span)
            source = integrals_ref.at[pl.ds(rows, rows), part]
            copy = pltpu.make_async_copy(source, bottom_ref.at[:, part], sems.at[len(copies)])
            copy.start()
            copies.append(copy)

    def both(ref):
        return partial_product(packed_ref, ref, core, x) + partial_product(swapped_ref, ref, 1 - core, x)

    @pl.when(core >= 0)
    def _():
        out_ref[:, pl.ds(0, rows)] = both(top_ref)

    for copy in copies[:2]:
        copy.wait()

    @pl.when(x >= 0)
    def _():
        out_ref[:, pl.ds(rows, rows)] = both(bottom_ref)

    for copy in copies[2:]:
        copy.wait()


def far_kernel(packed_ref, before_ref, top_ref, bottom_ref, out_ref):
    core, x = lax.axis_index("core"), X - 1 - lax.axis_index("x")
    out_ref[...] = before_ref[...] + product(packed_ref, top_ref, bottom_ref, core, x)


def last_kernel(packed_ref, before_ref, top_ref, bottom_ref, out_ref):
    core, x = 1 - lax.axis_index("core"), X - 1 - lax.axis_index("x")
    total = before_ref[...] + product(packed_ref, top_ref, bottom_ref, core, x)
    for j in range(out_ref.shape[0]):
        out_ref[j] = total


def finish_kernel(odd_ref, shared_ref, out_ref):
    odd = jnp.concatenate([odd_ref[...]] * (out_ref.shape[1] // odd_ref.shape[1]), axis=1) != 0
    sums = []
    for h in range(2):
        total = shared_ref[GROUP_ORDER.index(h * ROW)]
        for j in range(1, ROW):
            total = total + shared_ref[GROUP_ORDER.index(h * ROW + j)]
        sums.append(total)
    out_ref[...] = jnp.where(odd, sums[1], sums[0]).astype(out_ref.dtype)


def place_kernel(place_ref, block_ref, out_ref):
    block = block_ref[...].astype(jnp.float32)
    pairs, width = block.shape
    lower = lower_lanes(pairs)
    left = lower & (place_ref[0] != 0)
    right = jnp.logical_not(lower) & (place_ref[1] != 0)
    rows = []
    for j in range(width // (2 * TS)):
        part = block[:, j * 2 * TS : (j + 1) * 2 * TS]
        turned = pltpu.roll(part, TS, 1)
        rows.append(jnp.where(left, part, jnp.where(right, turned, 0.0)))
        rows.append(jnp.where(left, turned, jnp.where(right, part, 0.0)))
    out_ref[...] = jnp.swapaxes(jnp.stack(rows, 0), 0, 1).astype(out_ref.dtype)


def per_device(amplitudes, integrals, partner):
    pairs, rows_dev, _ = amplitudes.shape
    width = rows_dev * TS
    bra = integrals.shape[0]
    params = pltpu.CompilerParams(vmem_limit_bytes=4 * 1024 * 1024)
    sent, pick, odd, place = pl.pallas_call(
        prepare_kernel,
        out_shape=[
            pltpu.VMEM((TILES, pairs, width), jnp.bfloat16),
            pltpu.VMEM((2, TILES, pairs, 128), jnp.int32),
            pltpu.VMEM((pairs, 128), jnp.int32),
            pltpu.VMEM((2, pairs, 128), jnp.int32),
        ],
        in_specs=[HBM, HBM],
        out_specs=[VMEM, VMEM, VMEM, VMEM],
        scratch_shapes=[
            pltpu.SMEM(partner.shape, partner.dtype),
            pltpu.VMEM(amplitudes.shape, amplitudes.dtype),
            pltpu.SemaphoreType.DMA((2,)),
        ],
        compiler_params=params,
        name="prepare",
    )(in_hbm(partner), in_hbm(amplitudes))
    got = lax.all_to_all(sent, ("zh", "zl"), 0, 0, axis_index_groups=[list(Z_ORDER)], tiled=True)
    chosen = pl.pallas_call(
        choose_kernel,
        out_shape=pltpu.VMEM((2, pairs, width), jnp.bfloat16),
        in_specs=[VMEM, VMEM],
        out_specs=VMEM,
        compiler_params=params,
        name="choose",
    )(in_vmem(pick), in_vmem(got))
    staged = pltpu.VMEM((bra // 2, integrals.shape[1]), integrals.dtype)

    def local(kernel, shape, dtype, operands, cost=None, name=None, scratch=(), specs=None):
        return pl.pallas_call(
            kernel,
            out_shape=pltpu.VMEM(shape, dtype),
            in_specs=specs or [VMEM] * len(operands),
            out_specs=VMEM,
            scratch_shapes=scratch,
            compiler_params=params,
            cost_estimate=cost,
            name=name,
        )(*operands)

    def multiply(kernel, operands, name, copies=()):
        cost = pl.CostEstimate(
            flops=pairs * integrals.size // 2, bytes_accessed=integrals.size // 2, transcendentals=0
        )
        operands = [in_vmem(operand) for operand in operands]
        return local(kernel, (*copies, pairs, bra), jnp.float32, operands, cost, name)

    core_swap = [(0, 1), (1, 0)]
    beside = lax.ppermute(chosen, "x", [(i, i ^ 1) for i in range(X)])
    top = pl.pallas_call(
        stage_top_kernel,
        out_shape=staged,
        in_specs=[HBM],
        out_specs=VMEM,
        scratch_shapes=[pltpu.SemaphoreType.DMA((PIECES,))],
        compiler_params=params,
        cost_estimate=pl.CostEstimate(flops=0, bytes_accessed=2 * integrals.size, transcendentals=0),
        name="stage_top",
    )(in_hbm(integrals))
    couple = local(
        join_kernel,
        (2, 2, pairs, width),
        chosen.dtype,
        [in_vmem(chosen[None]), in_vmem(beside[None]), in_vmem(top)],
        name="join",
    )
    swapped = lax.ppermute(couple, "core", core_swap)
    across = lax.ppermute(couple, "x", [(i, X - 1 - i) for i in range(X)])
    bottom, total = pl.pallas_call(
        near_kernel,
        out_shape=[staged, pltpu.VMEM((pairs, bra), jnp.float32)],
        in_specs=[VMEM, VMEM, VMEM, HBM],
        out_specs=[VMEM, VMEM],
        scratch_shapes=[pltpu.SemaphoreType.DMA((PIECES,))],
        compiler_params=params,
        cost_estimate=pl.CostEstimate(
            flops=pairs * integrals.size, bytes_accessed=2 * integrals.size, transcendentals=0
        ),
        name="near_product",
    )(in_vmem(couple), in_vmem(swapped), in_vmem(top), in_hbm(integrals))
    across = local(after_kernel, across.shape, across.dtype, [in_vmem(across), in_vmem(total)], name="after")
    swapped = lax.ppermute(across, "core", core_swap)
    total = multiply(far_kernel, [across, total, top, bottom], "far_product")
    partials = multiply(last_kernel, [swapped, total, top, bottom], "last_product", (ZL * ROW,))
    shared = lax.all_to_all(partials, ("zl", "row"), 0, 0, axis_index_groups=[list(GROUP_ORDER)], tiled=True)
    block = pl.pallas_call(
        finish_kernel,
        out_shape=pltpu.VMEM((pairs, bra), jnp.bfloat16),
        in_specs=[VMEM, VMEM],
        out_specs=VMEM,
        compiler_params=params,
        name="finish",
    )(in_vmem(odd), in_vmem(shared))
    block = lax.ppermute(block, AXES, delivery_pairs())
    return pl.pallas_call(
        place_kernel,
        out_shape=jax.ShapeDtypeStruct(amplitudes.shape, jnp.bfloat16),
        in_specs=[VMEM, VMEM],
        out_specs=VMEM,
        compiler_params=params,
        name="place",
    )(in_vmem(place), in_vmem(block))


def solution(mesh):
    fine = Mesh(mesh.devices.reshape(ZH, ZL, X, CORE, ROW), AXES)
    col = ("zh", "zl", "x", "core")
    return jax.shard_map(
        per_device,
        mesh=fine,
        in_specs=(P(None, col, "row"), P(col, "row"), P()),
        out_specs=P(None, col, "row"),
        check_vma=False,
    )
```
